128 devices in a mesh: depth: 4 (over z), tile: 32 (over y, x, core).
Axes of the slice: x: 4, y: 4, z: 4, core: 2. Of those that a mesh axis runs over, the one named last changes fastest.
Arguments:
- features: bfloat16 [1024, 32, 512], P(('depth', 'tile')), may hold values from -6 to 6
- cotangent: bfloat16 [1024, 32, 512], P(('depth', 'tile')), may hold values from -6 to 6
- first_weight: bfloat16 [27, 32, 32], replicated, may hold values from -0.21875 to 0.21875
- second_weight: bfloat16 [27, 32, 32], replicated, may hold values from -0.21875 to 0.21875
- neighbours: int32 [1024, 26], P(('depth', 'tile')), may hold values from -1 to 15
- send_depth: int32 [128, 2, 2], P(('depth', 'tile')), may hold values from 0 to 7
- send_tile: int32 [128, 2, 2], P(('depth', 'tile')), may hold values from 0 to 11
- worker_tile: int32 [1024, 1], P(('depth', 'tile')), may hold values from 0 to 31; in each aligned block of 8 rows (0 to 7, 8 to 15, ...) at most 2 rows name the same one
Outputs:
- moved_grad: bfloat16 [8192, 32, 512], P(('depth', 'tile'))
- grad_weights: float32 [2, 27, 32, 32], replicated
The draws below stay inside these ranges and needn't reach their ends.
Inputs may be any that keep to these rules, and one draw needn't show every extreme that they name: `neighbours`: lookup entries, -1 where no active brick is at that offset. `send_depth`: brick slots of the sending device. `send_tile`: entries of the sending device's depth-section lookup. `worker_tile`: at most 2 bricks of one device name the same tile, and this is reached.
All inputs are finite; a program needn't handle non-finite values.
Results may differ from the reference program's by a relative error of at most 0.0032.
Values may be sent and summed in bfloat16 or wider, within the bound.
A program may use at most 256 MiB of HBM per device.

```python
import math
import jax
import jax.numpy as jnp
import numpy as np
from jax import lax

C = 32
BS = 8
NB = 8
CELLS = 512
HD = 2
HT = 2
TABLE = 16
Q = 2
SLOTS = 64
N_DEPTH = 4
N_TILE = 32
DEVICES = 128


def place_ends(array, key, smallest, top_value):
    dims = array.shape
    place = [jax.random.randint(jax.random.fold_in(key, axis), (), 0, dims[axis]) for axis in range(len(dims))]
    array = array.at[tuple(place)].set(smallest)
    longest = dims.index(max(dims))
    place[longest] = (place[longest] + 1) % dims[longest]
    return array.at[tuple(place)].set(top_value)


def shard_levels(rng, extent, pieces, smallest, high):
    def one(axis_at, blocks):
        draws = jax.random.uniform(jax.random.fold_in(jax.random.fold_in(rng, 6), axis_at), (blocks,), jnp.float32, smallest / len(pieces), high / len(pieces))
        return jnp.repeat(jnp.exp(draws), extent[axis_at] // blocks).reshape((-1,) + (1,) * (len(extent) - axis_at - 1))

    factor_of = one(*pieces[0])
    for cut in pieces[1:]:
        factor_of = factor_of * one(*cut)
    return factor_of


def routed_block(rng, own, number, rows, number_of, top, limit, lean):
    order = jax.random.permutation(rng, number_of)
    heavy_load, common = shares(number_of, rows * top, limit, lean, True), shares(number_of, rows * top, limit, lean, False)
    places = jnp.arange(number_of)

    def named(lengths, turn):
        used = int((lengths > 0).sum())
        fixed = max(1, used // 4)
        passed = fixed + (places - fixed + turn * (used - fixed)) % max(1, number_of - fixed)
        return jnp.zeros((number_of,), jnp.int32).at[order[jnp.where(places < fixed, places, passed)]].set(jnp.asarray(lengths, jnp.int32))

    lengths = jnp.where(number % 4 == 0, named(heavy_load, number // 4), named(common, number - number // 4 - 1))
    mixed = jax.random.permutation(jax.random.fold_in(own, 3), number_of)
    giver, taker = mixed[0:number_of // 2 * 2:2], mixed[1:number_of // 2 * 2:2]
    margin = jnp.minimum(lengths[giver] - 1, limit - lengths[taker]) // 2
    margin = jnp.where((giver == order[0]) | (taker == order[0]) | (lengths[taker] == 0), 0, jnp.maximum(margin, 0))
    passed = jax.random.randint(jax.random.fold_in(own, 4), (number_of // 2,), 0, 1 << 20) % (margin + 1)
    lengths = lengths.at[giver].add(-passed).at[taker].add(passed)
    items = jnp.searchsorted(jnp.cumsum(lengths), jnp.arange(rows * top), side="right").astype(jnp.int32)
    table = items.reshape(top, rows).T
    table = table[jax.random.permutation(jax.random.fold_in(own, 1), rows)]
    turn = jax.random.randint(jax.random.fold_in(own, 2), (rows, 1), 0, top)
    return jnp.take_along_axis(table, (jnp.arange(top)[None, :] + turn) % top, axis=1)


def shares(amount, total, reach, skew, full):
    portions = [(1 << 20) // math.isqrt(grade ** skew) + 1 for grade in range(1, amount + 1)]
    largest = reach if full else min(reach, max(-(-total // amount), total * portions[0] // sum(portions)))
    least = 1 if total - largest >= amount - 1 else 0
    counts, spare = [largest] + [least] * (amount - 1), total - largest - least * (amount - 1)
    while spare > 0:
        candidates = [i for i in range(1, amount) if counts[i] < largest] or [i for i in range(1, amount) if counts[i] < reach]
        whole, budget = sum([portions[i] for i in candidates]), spare
        for i in candidates:
            more = min(reach - counts[i], max(1, budget * portions[i] // whole), spare)
            counts[i] = counts[i] + more
            spare = spare - more
    return np.array(counts)


def scatter_about(rng, dims, deviation, reach, shards=(), kind=jnp.bfloat16):
    values = deviation * jax.random.normal(rng, dims, jnp.float32)
    if shards:
        values = values * shard_levels(rng, dims, shards, -0.22, 0.18)
    return jnp.clip(values, -reach, reach).astype(kind)


def setup_inputs(seed: int = 0) -> dict:
    keys = jax.random.split(jax.random.key(seed), 9)
    features = scatter_about(keys[0], (DEVICES * NB, C, CELLS), 1.0, 6.0, ((0, 128),))
    cotangent = scatter_about(keys[1], (DEVICES * NB, C, CELLS), 1.0, 6.0, ((0, 128),))
    first_weight = scatter_about(keys[2], (27, C, C), (27 * C) ** -0.5, 0.21875)
    second_weight = scatter_about(keys[3], (27, C, C), (27 * C) ** -0.5, 0.21875)
    neighbours = place_ends(jax.random.randint(keys[4], (DEVICES * NB, 26), -1, TABLE), jax.random.fold_in(keys[4], 1), -1, TABLE - 1).astype(jnp.int32)
    send_depth = place_ends(jax.random.randint(keys[5], (DEVICES, 2, HD), 0, NB), jax.random.fold_in(keys[5], 1), 0, NB - 1).astype(jnp.int32)
    send_tile = place_ends(jax.random.randint(keys[6], (DEVICES, 2, HT), 0, NB + 2 * HD), jax.random.fold_in(keys[6], 1), 0, (NB + 2 * HD) - 1).astype(jnp.int32)
    worker_tile_keys = jax.random.split(jax.random.fold_in(keys[7], 1), (DEVICES * NB) // NB)
    worker_tile_turns = jax.random.permutation(jax.random.fold_in(keys[7], 3), (DEVICES * NB) // NB)
    worker_tile = jax.vmap(lambda own, number: routed_block(jax.random.fold_in(keys[7], 2), own, number, NB, N_TILE, 1, Q, 2))(worker_tile_keys, worker_tile_turns).reshape((DEVICES * NB, 1))
    return dict(features=features, cotangent=cotangent, first_weight=first_weight, second_weight=second_weight, neighbours=neighbours, send_depth=send_depth, send_tile=send_tile, worker_tile=worker_tile)


def silu_grad(values):
    sigma = jax.nn.sigmoid(values)
    return sigma * (1.0 + values * (1.0 - sigma))

def pick_rows(source, indices):
    return jnp.take_along_axis(source, indices[..., None, None], axis=2)

def build_lookup(field_rows, send_depth, send_tile):
    stacked = field_rows.reshape(N_DEPTH, N_TILE, NB, C, CELLS)
    depth_lists = send_depth.reshape(N_DEPTH, N_TILE, 2, HD)
    to_lower = pick_rows(stacked, depth_lists[:, :, 0])
    to_upper = pick_rows(stacked, depth_lists[:, :, 1])
    nothing = jnp.zeros_like(to_lower[:1])
    from_lower = jnp.concatenate([nothing, to_upper[:-1]], 0)
    from_upper = jnp.concatenate([to_lower[1:], nothing], 0)
    section_one = jnp.concatenate([stacked, from_lower, from_upper], 2)
    tile_lists = send_tile.reshape(N_DEPTH, N_TILE, 2, HT)
    tile_lower = pick_rows(section_one, tile_lists[:, :, 0])
    tile_upper = pick_rows(section_one, tile_lists[:, :, 1])
    from_left = jnp.roll(tile_upper, 1, axis=1)
    from_right = jnp.roll(tile_lower, -1, axis=1)
    zero_brick = jnp.zeros_like(stacked[:, :, :1])
    lookup = jnp.concatenate([section_one, from_left, from_right, zero_brick], 2)
    return lookup.reshape(DEVICES, TABLE + 1, C, CELLS)

def neighbourhood(lookup, link_rows, self_rows):
    complete = jnp.concatenate([link_rows[:, :13], self_rows[:, None], link_rows[:, 13:]], 1)
    complete = jnp.where(complete < 0, lookup.shape[0] - 1, complete).astype(jnp.int32)
    bricks = jnp.take(lookup, complete, axis=0)
    rows = bricks.shape[0]
    channels = bricks.shape[2]
    bricks = bricks.reshape(rows, 3, 3, 3, channels, BS, BS, BS).transpose(0, 4, 1, 5, 2, 6, 3, 7)
    assembled = bricks.reshape(rows, channels, 3 * BS, 3 * BS, 3 * BS)
    return assembled[:, :, BS - 1:2 * BS + 1, BS - 1:2 * BS + 1, BS - 1:2 * BS + 1]

def shifted(padded, k):
    a, b, c = (k // 9, k // 3 % 3, k % 3)
    return padded[:, :, a:a + BS, b:b + BS, c:c + BS].reshape(padded.shape[0], padded.shape[1], BS ** 3)

def reference(features, cotangent, first_weight, second_weight, neighbours, send_depth, send_tile, worker_tile):
    highest = lax.Precision.HIGHEST
    link_all = neighbours.reshape(DEVICES, NB, 26)
    self_rows = jnp.arange(NB, dtype=jnp.int32)
    first_w = first_weight.astype(jnp.float32)
    second_w = second_weight.astype(jnp.float32)
    input_lookup = build_lookup(features, send_depth, send_tile)

    def conv_forward(item):
        lookup, link_rows = item
        padded = neighbourhood(lookup, link_rows, self_rows).astype(jnp.float32)
        result = jnp.zeros((NB, C, CELLS), jnp.float32)
        for k in range(27):
            result = result + jnp.einsum('nim,io->nom', shifted(padded, k), first_w[k], precision=highest)
        return result
    pre_act = lax.map(conv_forward, (input_lookup, link_all))
    hidden = jax.nn.silu(pre_act).astype(jnp.bfloat16)
    grad_lookup = build_lookup(cotangent, send_depth, send_tile)

    def second_pass(item):
        lookup, link_rows, hidden_rows = item
        padded = neighbourhood(lookup, link_rows, self_rows).astype(jnp.float32)
        hidden_wide = hidden_rows.astype(jnp.float32)
        result = jnp.zeros((NB, C, CELLS), jnp.float32)
        parts = []
        for k in range(27):
            piece = shifted(padded, 26 - k)
            result = result + jnp.einsum('nom,io->nim', piece, second_w[k], precision=highest)
            parts.append(jnp.einsum('nim,nom->io', hidden_wide, piece, precision=highest))
        return (result, jnp.stack(parts))
    grad_hidden, second_parts = lax.map(second_pass, (grad_lookup, link_all, hidden))
    grad_pre = (grad_hidden * silu_grad(pre_act)).astype(jnp.bfloat16)
    pre_lookup = build_lookup(grad_pre.reshape(DEVICES * NB, C, CELLS), send_depth, send_tile)

    def third_pass(item):
        lookup, link_rows, input_rows = item
        padded = neighbourhood(lookup, link_rows, self_rows).astype(jnp.float32)
        input_wide = input_rows.astype(jnp.float32)
        result = jnp.zeros((NB, C, CELLS), jnp.float32)
        parts = []
        for k in range(27):
            piece = shifted(padded, 26 - k)
            result = result + jnp.einsum('nom,io->nim', piece, first_w[k], precision=highest)
            parts.append(jnp.einsum('nim,nom->io', input_wide, piece, precision=highest))
        return (result, jnp.stack(parts))
    conv_back, first_parts = lax.map(third_pass, (pre_lookup, link_all, features.reshape(DEVICES, NB, C, CELLS)))
    grad_input = (cotangent.reshape(DEVICES, NB, C, CELLS).astype(jnp.float32) + conv_back).astype(jnp.bfloat16)
    factor = float(DEVICES * NB * CELLS) ** (-0.5)
    grad_weights = jnp.stack([lax.optimization_barrier(jnp.sum(first_parts, 0)), lax.optimization_barrier(jnp.sum(second_parts, 0))]) * factor
    worker_rows = worker_tile.reshape(N_DEPTH, N_TILE, NB)
    onehot = (worker_rows[..., None] == jnp.arange(N_TILE, dtype=jnp.int32)).astype(jnp.int32)
    before = jnp.cumsum(onehot, axis=2) - onehot
    rank = lax.optimization_barrier(jnp.sum(before * onehot, -1)).astype(jnp.int32)
    depth_index = jnp.arange(N_DEPTH, dtype=jnp.int32)[:, None, None]
    tile_index = jnp.arange(N_TILE, dtype=jnp.int32)[None, :, None]
    target = (((depth_index * N_TILE + worker_rows) * N_TILE + tile_index) * Q + rank).astype(jnp.int32)
    moved_grad = jnp.zeros((DEVICES * SLOTS, C, CELLS), jnp.bfloat16)
    moved_grad = moved_grad.at[target.reshape(-1)].set(grad_input.reshape(DEVICES * NB, C, CELLS))
    return (moved_grad, grad_weights)
```

```python
import jax
import jax.numpy as jnp
from jax import lax
from jax.experimental import pallas as pl
from jax.experimental.pallas import tpu as pltpu
from jax.sharding import PartitionSpec as P

F32 = jnp.float32
BF16 = jnp.bfloat16


def iota(shape, dim):
    return lax.broadcasted_iota(jnp.int32, shape, dim)


def tiled_identity(lanes):
    return jnp.where(iota((32, lanes), 1) % 32 == iota((32, lanes), 0), 1.0, 0.0).astype(BF16)


def fill_table(table, slot, brick):
    spread = lax.dot_general(brick, tiled_identity(128), (((0,), (0,)), ((), ())), preferred_element_type=F32)
    table[slot] = spread.reshape(64, 8, 128)


def spread_weight(weight, wide):
    columns = iota((32, 256), 1) // 32
    rows = jnp.dot(weight[...].reshape(864, 32), tiled_identity(256), preferred_element_type=F32).astype(BF16)
    for k in range(27):
        for n in range(8):
            part = jnp.where(columns == n, rows[32 * k : 32 * k + 32], jnp.zeros((), BF16))
            wide[k // 9, pl.ds(256 * (k % 9) + 32 * n, 32), :] = part


def build_shifts(table, links, even, odd):
    lane = iota((8, 128), 1)
    sub = iota((8, 128), 0)

    def one_plane(a_block, a_source, a_row):
        entry = {}
        for rest in range(9):
            k = a_block * 9 + rest
            for n in range(8):
                if k == 13:
                    entry[rest, n] = n
                else:
                    link = links[n, k - (k > 13)]
                    entry[rest, n] = jnp.where(link < 0, 16, link)

        for half in range(2):
            def mixed(rest, b_source):
                parts = [table[entry[rest, 4 * half + j], a_source * 8 + b_source] for j in range(4)]
                low = jnp.where(lane < 32, parts[0], parts[1])
                high = jnp.where(lane < 96, parts[2], parts[3])
                return jnp.where(lane < 64, low, high)

            columns = pl.ds(128 * half, 128)
            rows = []
            for b in range(10):
                b_block, b_source = (b + 7) // 8, (b + 7) % 8
                mid = mixed(b_block * 3 + 1, b_source)
                lower = mixed(b_block * 3, b_source)
                upper = mixed(b_block * 3 + 2, b_source)
                down = pltpu.roll(jnp.where(sub == 7, lower, mid), 1, 0)
                up = pltpu.roll(jnp.where(sub == 0, upper, mid), 7, 0)
                rows.append((down, mid, up))
                if b > 0:
                    for v in range(3):
                        pair = jnp.concatenate([rows[b - 1][v], rows[b][v]], 0).astype(BF16)
                        if b % 2:
                            even[v, a_row, pl.ds(8 * (b - 1), 16), columns] = pair
                        else:
                            odd[v, a_row, pl.ds(8 * (b - 2), 16), columns] = pair

    one_plane(0, 7, 0)

    def middle(a, carry):
        one_plane(1, a, a + 1)
        return carry

    lax.fori_loop(0, 8, middle, 0)
    one_plane(2, 0, 9)


def piece(even, odd, a, rest):
    b, c = rest // 3, rest % 3
    source = odd[c, pl.ds(a, 8)] if b == 1 else even[c, pl.ds(a, 8), pl.ds(8 * b, 64)]
    return source.reshape(512, 256)


def conv_forward(even, odd, wide, total):
    def step(a, carry):
        left = jnp.concatenate([piece(even, odd, a, rest) for rest in range(9)], 1)
        total[...] += jnp.dot(left, wide[a], preferred_element_type=F32)
        return carry

    lax.fori_loop(0, 3, step, 0)


def conv_backward(even, odd, wide, total):
    def step(a, carry):
        acc = total[...]
        for rest in range(9):
            acc += lax.dot_general(
                piece(even, odd, a, rest), wide[2 - a, pl.ds(256 * (8 - rest), 256), :], (((1,), (1,)), ((), ())), preferred_element_type=F32
            )
        total[...] = acc
        return carry

    lax.fori_loop(0, 3, step, 0)


def weight_gradient(left_of, even, odd, folded):
    lane = iota((32, 128), 1)

    def step(a, carry):
        for rest in range(9):
            full = jnp.dot(left_of(), piece(even, odd, a, rest), preferred_element_type=F32)
            halves = []
            for half in range(2):
                parts = [full[128 * half + 32 * j : 128 * half + 32 * j + 32, 128 * half : 128 * half + 128] for j in range(4)]
                low = jnp.where(lane < 32, parts[0], parts[1])
                high = jnp.where(lane < 96, parts[2], parts[3])
                halves.append(jnp.where(lane < 64, low, high))
            both = halves[0] + halves[1]
            both = both + pltpu.roll(both, 64, 1)
            both = both + pltpu.roll(both, 32, 1)
            folded[pl.ds(pl.multiple_of(32 * (9 * (2 - a) + 8 - rest), 32), 32), :] = both
        return carry

    lax.fori_loop(0, 3, step, 0)


def pack_gradient(folded, packed):
    lane = iota((8, 128), 1)
    for r in range(27):
        parts = [folded[pl.ds(8 * (27 * g + r), 8), :] for g in range(4)]
        low = jnp.where(lane < 32, parts[0], parts[1])
        high = jnp.where(lane < 96, parts[2], parts[3])
        packed[r] = jnp.where(lane < 64, low, high)
    packed[27:32] = jnp.zeros((5, 8, 128), F32)

MESH = pl.DeviceIdType.MESH
DEPTHS, TILES = 4, 32


def remote(source, target, send, receive, device):
    return pltpu.make_async_remote_copy(
        src_ref=source, dst_ref=target, send_sem=send, recv_sem=receive, device_id=device, device_id_type=MESH
    )


def place():
    d, t = lax.axis_index("depth"), lax.axis_index("tile")
    return d, t, (t // 2) * 2, t % 2


def greet():
    d, t, chip, core = place()
    barrier = pltpu.get_barrier_semaphore()

    def tile_peer(i, carry):
        pl.semaphore_signal(barrier, inc=1, device_id=(d, (t + i) % TILES), device_id_type=MESH)
        return carry

    def depth_peer(i, carry):
        other = ((d + 1 + i // 2) % DEPTHS, chip + i % 2)
        pl.semaphore_signal(barrier, inc=1, device_id=other, device_id_type=MESH)
        return carry

    lax.fori_loop(1, TILES, tile_peer, 0)
    lax.fori_loop(0, 2 * (DEPTHS - 1), depth_peer, 0)
    return barrier


def depth_copies(stage, land, sends, receives):
    d, t, _, _ = place()
    return (
        remote(stage.at[0], land.at[1], sends.at[0], receives.at[1], ((d + DEPTHS - 1) % DEPTHS, t)),
        remote(stage.at[1], land.at[0], sends.at[1], receives.at[0], ((d + 1) % DEPTHS, t)),
    )


def tile_copies(stage, land, sends, receives):
    d, t, _, _ = place()
    return (
        remote(stage.at[0], land.at[1], sends.at[0], receives.at[1], (d, (t + TILES - 1) % TILES)),
        remote(stage.at[1], land.at[0], sends.at[1], receives.at[0], (d, (t + 1) % TILES)),
    )


def stage_depth(fields, send_depth, stage):
    for side in range(2):
        for f, field in enumerate(fields):
            for j in range(2):
                stage[side, 2 * f + j] = field[send_depth[0, side, j]]


def accept_depth(fields, land, sections, tables):
    d, _, _, _ = place()
    inner = (d > 0, d < DEPTHS - 1)
    for f, field in enumerate(fields):
        sections[f, 0:8] = field[...]
        for side in range(2):
            for j in range(2):
                value = land[side, 2 * f + j]
                value = jnp.where(inner[side], value, jnp.zeros_like(value))
                sections[f, 8 + 2 * side + j] = value


def stage_tile(count, sections, send_tile, stage):
    for side in range(2):
        for f in range(count):
            for j in range(2):
                stage[side, 2 * f + j] = sections[f, send_tile[0, side, j]]


def table_own(fields, tables):
    for field, table in zip(fields, tables):
        for m in range(8):
            fill_table(table, m, field[m])


def table_depth(sections, tables):
    for f, table in enumerate(tables):
        for j in range(4):
            fill_table(table, 8 + j, sections[f, 8 + j])


def table_tile(land, tables):
    for f, table in enumerate(tables):
        for side in range(2):
            for j in range(2):
                fill_table(table, 12 + 2 * side + j, land[side, 2 * f + j])


def ring_copy(i, source, target, sends, receives, group):
    d, t, chip, core = place()
    if group == 8:
        me = d * 2 + core
        peer = (me + i) % 8
        device = (peer // 2, chip + peer % 2)
    elif group == 16:
        me = t // 2
        peer = (me + i) % 16
        device = (d, 2 * peer + core)
    else:
        me = t
        peer = (t + i) % TILES
        device = (d, peer)
    return remote(source(me, peer), target(me, peer), sends.at[peer], receives.at[me], device)


def arrived_copy(i, source, target, sends, receives, group):
    d, t, chip, core = place()
    if group == 8:
        me = d * 2 + core
        peer = (me + i) % 8
        device = (peer // 2, chip + peer % 2)
    elif group == 16:
        me = t // 2
        peer = (me + i) % 16
        device = (d, 2 * peer + core)
    else:
        me = t
        peer = (t + i) % TILES
        device = (d, peer)
    return remote(source(me, peer), target(peer, me), sends.at[peer], receives.at[peer], device)


def start_all(*args):
    def step(i, carry):
        ring_copy(i, *args).start()
        return carry

    lax.fori_loop(1, args[-1], step, 0)


def wait_arrived(*args):
    def step(i, carry):
        arrived_copy(i, *args).wait_recv()
        return carry

    lax.fori_loop(1, args[-1], step, 0)


def wait_sent(*args):
    def step(i, carry):
        ring_copy(i, *args).wait_send()
        return carry

    lax.fori_loop(1, args[-1], step, 0)


def reduce_plans(packed, land_a, part, land_b, result, sems):
    a_send, a_receive, b_send, b_receive, c_send, c_receive = sems
    first = (lambda me, peer: packed.at[pl.ds(4 * peer, 4)], lambda me, peer: land_a.at[me], a_send, a_receive, 8)
    second = (lambda me, peer: part, lambda me, peer: land_b.at[me], b_send, b_receive, 16)
    third = (lambda me, peer: land_b.at[16], lambda me, peer: result.at[pl.ds(4 * me, 4)], c_send, c_receive, 8)
    return first, second, third


def reduce_first(plans, packed, land_a, part, land_b):
    d, t, chip, core = place()
    me = d * 2 + core
    wait_arrived(*plans[0])
    land_a[me] = packed[pl.ds(4 * me, 4)]
    total = land_a[0]
    for j in range(1, 8):
        total += land_a[j]
    part[...] = total
    land_b[t // 2] = total
    start_all(*plans[1])


def reduce_second(plans, part, land_b, result, factor):
    d, t, chip, core = place()
    me = d * 2 + core
    wait_arrived(*plans[1])
    total = land_b[0]
    for j in range(1, 16):
        total += land_b[j]
    total = total * factor
    land_b[16] = total
    result[pl.ds(4 * me, 4)] = total
    start_all(*plans[2])


def unpack_gradient(result, out, w):
    for r in range(27):
        tile = result[r]
        for g in range(4):
            t = 27 * g + r
            moved = tile if g == 0 else pltpu.roll(tile, 128 - 32 * g, 1)
            out[w, t // 4, pl.ds(8 * (t % 4), 8), :] = moved[:, :32]


def kernel(
    features, cotangent, first_weight, second_weight, links, send_depth, send_tile, workers,
    moved, gradients,
    table_x, table_g, even_x, odd_x, even_g, odd_g, wide_first, wide_second, pre, back, hidden, folded,
    grad_pre, grad_input, outgoing,
    stage_d, land_d, stage_t, land_t, sections,
    stage_d2, land_d2, stage_t2, land_t2, sections2,
    packed, land_a, part, land_b, result,
    d_send, d_receive, t_send, t_receive, d2_send, d2_receive, t2_send, t2_receive,
    m_send, m_receive, own_sem, a_send, a_receive, b_send, b_receive, c_send, c_receive,
):
    d, t, chip, core = place()
    fields, tables = (features, cotangent), (table_x, table_g)
    barrier = greet()
    stage_depth(fields, send_depth, stage_d)
    pl.semaphore_wait(barrier, TILES - 1 + 2 * (DEPTHS - 1))
    along_depth = depth_copies(stage_d, land_d, d_send, d_receive)
    for copy in along_depth:
        copy.start()
    table_own(fields, tables)
    table_x[16] = jnp.zeros((64, 8, 128), F32)
    table_g[16] = jnp.zeros((64, 8, 128), F32)
    for copy in along_depth:
        copy.wait()
    accept_depth(fields, land_d, sections, tables)
    stage_tile(2, sections, send_tile, stage_t)
    along_tile = tile_copies(stage_t, land_t, t_send, t_receive)
    for copy in along_tile:
        copy.start()
    table_depth(sections, tables)
    spread_weight(first_weight, wide_first)
    spread_weight(second_weight, wide_second)
    for copy in along_tile:
        copy.wait()
    table_tile(land_t, tables)
    build_shifts(table_x, links, even_x, odd_x)
    build_shifts(table_g, links, even_g, odd_g)
    pre[...] = jnp.zeros((512, 256), F32)
    back[...] = jnp.zeros((512, 256), F32)
    conv_forward(even_x, odd_x, wide_first, pre)
    conv_backward(even_g, odd_g, wide_second, back)
    value = pre[...]
    sigma = 1.0 / (1.0 + jnp.exp(-value))
    hidden[...] = (value * sigma).T.astype(BF16)
    grad_pre[...] = (back[...] * sigma * (1.0 + value * (1.0 - sigma))).T.astype(BF16).reshape(8, 32, 512)

    stage_depth((grad_pre,), send_depth, stage_d2)
    along_depth = depth_copies(stage_d2, land_d2, d2_send, d2_receive)
    for copy in along_depth:
        copy.start()
    weight_gradient(lambda: hidden[...], even_g, odd_g, folded)
    for copy in along_depth:
        copy.wait()
    accept_depth((grad_pre,), land_d2, sections2, tables)
    stage_tile(1, sections2, send_tile, stage_t2)
    along_tile = tile_copies(stage_t2, land_t2, t2_send, t2_receive)
    for copy in along_tile:
        copy.start()
    pack_gradient(folded, packed.at[1])
    plans = [
        reduce_plans(
            packed.at[w], land_a.at[w], part.at[w], land_b.at[w], result.at[w],
            tuple(s.at[w] for s in (a_send, a_receive, b_send, b_receive, c_send, c_receive)),
        )
        for w in range(2)
    ]
    start_all(*plans[1][0])
    table_own((grad_pre,), tables[:1])
    table_depth(sections2, tables[:1])
    for copy in along_tile:
        copy.wait()
    table_tile(land_t2, tables[:1])
    build_shifts(table_x, links, even_x, odd_x)
    back[...] = jnp.zeros((512, 256), F32)
    conv_backward(even_x, odd_x, wide_first, back)
    grad_input[0:8] = (back[...].T.reshape(8, 32, 512) + cotangent[...].astype(F32)).astype(BF16)
    grad_input[8] = jnp.zeros((32, 512), BF16)

    names = [workers[n, 0] for n in range(8)]
    slots = []
    for n in range(8):
        rank = jnp.int32(0)
        for m in range(n):
            rank = rank + jnp.where(names[m] == names[n], 1, 0)
        slots.append(2 * names[n] + rank)

    def place_brick(s, carry):
        brick = jnp.int32(8)
        for n in range(8):
            brick = jnp.where(slots[n] == s, n, brick)
        outgoing[s] = grad_input[brick]
        return carry

    lax.fori_loop(0, 2 * TILES, place_brick, 0)
    own = pltpu.make_async_copy(outgoing.at[pl.ds(2 * t, 2)], moved.at[pl.ds(2 * t, 2)], own_sem)
    own.start()
    moves = (
        lambda me, peer: outgoing.at[pl.ds(2 * peer, 2)],
        lambda me, peer: moved.at[pl.ds(2 * me, 2)],
        m_send, m_receive, TILES,
    )
    start_all(*moves)

    factor = float(DEPTHS * TILES * 8 * 512) ** (-0.5)
    reduce_first(plans[1], packed.at[1], land_a.at[1], part.at[1], land_b.at[1])
    weight_gradient(lambda: features[...].reshape(256, 512), even_x, odd_x, folded)
    pack_gradient(folded, packed.at[0])
    start_all(*plans[0][0])
    reduce_second(plans[1], part.at[1], land_b.at[1], result.at[1], factor)
    reduce_first(plans[0], packed.at[0], land_a.at[0], part.at[0], land_b.at[0])
    wait_arrived(*plans[1][2])
    unpack_gradient(result.at[1], gradients, 1)
    reduce_second(plans[0], part.at[0], land_b.at[0], result.at[0], factor)
    wait_arrived(*plans[0][2])
    unpack_gradient(result.at[0], gradients, 0)
    for w in range(2):
        for plan in plans[w]:
            wait_sent(*plan)
    own.wait()
    wait_arrived(*moves)
    wait_sent(*moves)


def local(features, cotangent, first_weight, second_weight, neighbours, send_depth, send_tile, worker_tile):
    vmem, smem = pl.BlockSpec(memory_space=pltpu.VMEM), pl.BlockSpec(memory_space=pltpu.SMEM)
    brick = (32, 512)
    shifts = [pltpu.VMEM((3, 10, 80, 256), BF16), pltpu.VMEM((3, 10, 64, 256), BF16)]

    def halo(count):
        return [pltpu.VMEM((2, 2 * count, *brick), BF16)] * 4 + [pltpu.VMEM((count, 12, *brick), BF16)]

    dma = pltpu.SemaphoreType.DMA
    return pl.pallas_call(
        kernel,
        out_shape=(
            jax.ShapeDtypeStruct((2 * TILES, *brick), BF16),
            jax.ShapeDtypeStruct((2, 27, 32, 32), F32),
        ),
        in_specs=[vmem] * 4 + [smem] * 4,
        out_specs=(pl.BlockSpec(memory_space=pl.ANY), vmem),
        scratch_shapes=[pltpu.VMEM((17, 64, 8, 128), F32)] * 2
        + shifts * 2
        + [pltpu.VMEM((3, 2304, 256), BF16)] * 2
        + [pltpu.VMEM((512, 256), F32)] * 2
        + [pltpu.VMEM((256, 512), BF16), pltpu.VMEM((864, 128), F32)]
        + [pltpu.VMEM((8, *brick), BF16), pltpu.VMEM((9, *brick), BF16), pltpu.VMEM((64, *brick), BF16)]
        + halo(2)
        + halo(1)
        + [
            pltpu.VMEM((2, 32, 8, 128), F32),
            pltpu.VMEM((2, 8, 4, 8, 128), F32),
            pltpu.VMEM((2, 4, 8, 128), F32),
            pltpu.VMEM((2, 17, 4, 8, 128), F32),
            pltpu.VMEM((2, 32, 8, 128), F32),
        ]
        + [dma((2,))] * 8
        + [dma((TILES,))] * 2
        + [dma]
        + [dma((2, 8))] * 2
        + [dma((2, 16))] * 2
        + [dma((2, 8))] * 2,
        compiler_params=pltpu.CompilerParams(
            collective_id=0, has_side_effects=True, vmem_limit_bytes=50 * 2**20
        ),
    )(features, cotangent, first_weight, second_weight, neighbours, send_depth, send_tile, worker_tile)


def solution(mesh):
    rows = P(("depth", "tile"))
    placed = (rows, rows, P(), P(), rows, rows, rows, rows)
    return jax.shard_map(local, mesh=mesh, in_specs=placed, out_specs=(rows, P()), check_vma=False)
```

```python
import jax
import jax.numpy as jnp
from jax import lax
from jax.experimental import pallas as pl
from jax.experimental.pallas import tpu as pltpu
from jax.sharding import PartitionSpec as P

F32 = jnp.float32
BF16 = jnp.bfloat16


def iota(shape, dim):
    return lax.broadcasted_iota(jnp.int32, shape, dim)


def tiled_identity(lanes):
    return jnp.where(iota((32, lanes), 1) % 32 == iota((32, lanes), 0), 1.0, 0.0).astype(BF16)


def fill_table(table, slot, brick):
    spread = lax.dot_general(brick, tiled_identity(128), (((0,), (0,)), ((), ())), preferred_element_type=F32)
    table[slot] = spread.reshape(64, 8, 128)


def spread_weight(weight, wide):
    columns = iota((32, 256), 1) // 32
    rows = jnp.dot(weight[...].reshape(864, 32), tiled_identity(256), preferred_element_type=F32).astype(BF16)
    for k in range(27):
        for n in range(8):
            part = jnp.where(columns == n, rows[32 * k : 32 * k + 32], jnp.zeros((), BF16))
            wide[k // 9, pl.ds(256 * (k % 9) + 32 * n, 32), :] = part


def build_shifts(table, links, even, odd):
    lane = iota((8, 128), 1)
    sub = iota((8, 128), 0)

    def one_plane(a_block, a_source, a_row):
        entry = {}
        for rest in range(9):
            k = a_block * 9 + rest
            for n in range(8):
                if k == 13:
                    entry[rest, n] = n
                else:
                    link = links[n, k - (k > 13)]
                    entry[rest, n] = jnp.where(link < 0, 16, link)

        for half in range(2):
            def mixed(rest, b_source):
                parts = [table[entry[rest, 4 * half + j], a_source * 8 + b_source] for j in range(4)]
                low = jnp.where(lane < 32, parts[0], parts[1])
                high = jnp.where(lane < 96, parts[2], parts[3])
                return jnp.where(lane < 64, low, high)

            columns = pl.ds(128 * half, 128)
            rows = []
            for b in range(10):
                b_block, b_source = (b + 7) // 8, (b + 7) % 8
                mid = mixed(b_block * 3 + 1, b_source)
                lower = mixed(b_block * 3, b_source)
                upper = mixed(b_block * 3 + 2, b_source)
                down = pltpu.roll(jnp.where(sub == 7, lower, mid), 1, 0)
                up = pltpu.roll(jnp.where(sub == 0, upper, mid), 7, 0)
                rows.append((down, mid, up))
                if b > 0:
                    for v in range(3):
                        pair = jnp.concatenate([rows[b - 1][v], rows[b][v]], 0).astype(BF16)
                        if b % 2:
                            even[v, a_row, pl.ds(8 * (b - 1), 16), columns] = pair
                        else:
                            odd[v, a_row, pl.ds(8 * (b - 2), 16), columns] = pair

    one_plane(0, 7, 0)

    def middle(a, carry):
        one_plane(1, a, a + 1)
        return carry

    lax.fori_loop(0, 8, middle, 0)
    one_plane(2, 0, 9)


def piece(even, odd, a, rest):
    b, c = rest // 3, rest % 3
    source = odd[c, pl.ds(a, 8)] if b == 1 else even[c, pl.ds(a, 8), pl.ds(8 * b, 64)]
    return source.reshape(512, 256)


def conv_forward(even, odd, wide, total):
    def step(a, carry):
        left = jnp.concatenate([piece(even, odd, a, rest) for rest in range(9)], 1)
        total[...] += jnp.dot(left, wide[a], preferred_element_type=F32)
        return carry

    lax.fori_loop(0, 3, step, 0)


def conv_backward(even, odd, wide, total):
    def step(a, carry):
        acc = total[...]
        for rest in range(9):
            acc += lax.dot_general(
                piece(even, odd, a, rest), wide[2 - a, pl.ds(256 * (8 - rest), 256), :], (((1,), (1,)), ((), ())), preferred_element_type=F32
            )
        total[...] = acc
        return carry

    lax.fori_loop(0, 3, step, 0)


def weight_gradient(left_of, even, odd, folded):
    lane = iota((32, 128), 1)

    def step(a, carry):
        for rest in range(9):
            full = jnp.dot(left_of(), piece(even, odd, a, rest), preferred_element_type=F32)
            halves = []
            for half in range(2):
                parts = [full[128 * half + 32 * j : 128 * half + 32 * j + 32, 128 * half : 128 * half + 128] for j in range(4)]
                low = jnp.where(lane < 32, parts[0], parts[1])
                high = jnp.where(lane < 96, parts[2], parts[3])
                halves.append(jnp.where(lane < 64, low, high))
            both = halves[0] + halves[1]
            both = both + pltpu.roll(both, 64, 1)
            both = both + pltpu.roll(both, 32, 1)
            folded[pl.ds(pl.multiple_of(32 * (9 * (2 - a) + 8 - rest), 32), 32), :] = both
        return carry

    lax.fori_loop(0, 3, step, 0)


def pack_gradient(folded, packed):
    lane = iota((8, 128), 1)
    for r in range(27):
        parts = [folded[pl.ds(8 * (27 * g + r), 8), :] for g in range(4)]
        low = jnp.where(lane < 32, parts[0], parts[1])
        high = jnp.where(lane < 96, parts[2], parts[3])
        packed[r] = jnp.where(lane < 64, low, high)
    packed[27:32] = jnp.zeros((5, 8, 128), F32)

MESH = pl.DeviceIdType.MESH
DEPTHS, TILES = 4, 32


def remote(source, target, send, receive, device):
    return pltpu.make_async_remote_copy(
        src_ref=source, dst_ref=target, send_sem=send, recv_sem=receive, device_id=device, device_id_type=MESH
    )


def place():
    d, t = lax.axis_index("depth"), lax.axis_index("tile")
    return d, t, (t // 2) * 2, t % 2


def greet():
    d, t, chip, core = place()
    barrier = pltpu.get_barrier_semaphore()

    def tile_peer(i, carry):
        pl.semaphore_signal(barrier, inc=1, device_id=(d, (t + i) % TILES), device_id_type=MESH)
        return carry

    def depth_peer(i, carry):
        other = ((d + 1 + i // 2) % DEPTHS, chip + i % 2)
        pl.semaphore_signal(barrier, inc=1, device_id=other, device_id_type=MESH)
        return carry

    lax.fori_loop(1, TILES, tile_peer, 0)
    lax.fori_loop(0, 2 * (DEPTHS - 1), depth_peer, 0)
    return barrier


def depth_copies(stage, land, sends, receives):
    d, t, _, _ = place()
    return (
        remote(stage.at[0], land.at[1], sends.at[0], receives.at[1], ((d + DEPTHS - 1) % DEPTHS, t)),
        remote(stage.at[1], land.at[0], sends.at[1], receives.at[0], ((d + 1) % DEPTHS, t)),
    )


def tile_copies(stage, land, sends, receives):
    d, t, _, _ = place()
    return (
        remote(stage.at[0], land.at[1], sends.at[0], receives.at[1], (d, (t + TILES - 1) % TILES)),
        remote(stage.at[1], land.at[0], sends.at[1], receives.at[0], (d, (t + 1) % TILES)),
    )


def stage_depth(fields, send_depth, stage):
    for side in range(2):
        for f, field in enumerate(fields):
            for j in range(2):
                stage[side, 2 * f + j] = field[send_depth[0, side, j]]


def accept_depth(fields, land, sections, tables):
    d, _, _, _ = place()
    inner = (d > 0, d < DEPTHS - 1)
    for f, field in enumerate(fields):
        sections[f, 0:8] = field[...]
        for side in range(2):
            for j in range(2):
                value = land[side, 2 * f + j]
                value = jnp.where(inner[side], value, jnp.zeros_like(value))
                sections[f, 8 + 2 * side + j] = value


def stage_tile(count, sections, send_tile, stage):
    for side in range(2):
        for f in range(count):
            for j in range(2):
                stage[side, 2 * f + j] = sections[f, send_tile[0, side, j]]


def table_own(fields, tables):
    for field, table in zip(fields, tables):
        for m in range(8):
            fill_table(table, m, field[m])


def table_depth(sections, tables):
    for f, table in enumerate(tables):
        for j in range(4):
            fill_table(table, 8 + j, sections[f, 8 + j])


def table_tile(land, tables):
    for f, table in enumerate(tables):
        for side in range(2):
            for j in range(2):
                fill_table(table, 12 + 2 * side + j, land[side, 2 * f + j])


ORDER = (
    (1, 2, 1), (3, 1, 0), (0, 3, 1), (2, 2, 0), (0, 0, 1), (1, 3, 0),
    (3, 1, 1), (1, 0, 0), (2, 2, 1), (0, 1, 0), (1, 3, 1), (3, 2, 0),
    (1, 0, 1), (2, 3, 0), (0, 1, 1), (2, 0, 0), (3, 2, 1), (1, 1, 0),
    (2, 3, 1), (0, 2, 0), (2, 0, 1), (3, 3, 0), (1, 1, 1), (3, 0, 0),
    (0, 2, 1), (2, 1, 0), (3, 3, 1), (1, 2, 0), (3, 0, 1), (0, 3, 0),
    (2, 1, 1),
)


def shifted_tile(i, sign):
    t = lax.axis_index("tile")
    dy, dx, dc = ORDER[i]
    y, x, core = t // 8, (t // 2) % 4, t % 2
    return ((y + sign * dy + 4) % 4) * 8 + ((x + sign * dx + 4) % 4) * 2 + (core + dc) % 2


def move(i, outgoing, moved, sends, receives):
    d, t = lax.axis_index("depth"), lax.axis_index("tile")
    peer = shifted_tile(i, 1)
    return remote(outgoing.at[pl.ds(2 * peer, 2)], moved.at[pl.ds(2 * t, 2)], sends.at[i], receives.at[i], (d, peer))


def landed(i, outgoing, moved, sends, receives):
    d = lax.axis_index("depth")
    peer = shifted_tile(i, -1)
    return remote(outgoing.at[pl.ds(2 * peer, 2)], moved.at[pl.ds(2 * peer, 2)], sends.at[i], receives.at[i], (d, peer))


def ring_copy(i, source, target, sends, receives, group):
    d, t, chip, core = place()
    if group == 8:
        me = d * 2 + core
        peer = (me + i) % 8
        device = (peer // 2, chip + peer % 2)
    elif group == 16:
        me = t // 2
        peer = (me + i) % 16
        device = (d, 2 * peer + core)
    else:
        me = t
        peer = (t + i) % TILES
        device = (d, peer)
    return remote(source(me, peer), target(me, peer), sends.at[peer], receives.at[me], device)


def arrived_copy(i, source, target, sends, receives, group):
    d, t, chip, core = place()
    if group == 8:
        me = d * 2 + core
        peer = (me + i) % 8
        device = (peer // 2, chip + peer % 2)
    elif group == 16:
        me = t // 2
        peer = (me + i) % 16
        device = (d, 2 * peer + core)
    else:
        me = t
        peer = (t + i) % TILES
        device = (d, peer)
    return remote(source(me, peer), target(peer, me), sends.at[peer], receives.at[peer], device)


def start_all(*args):
    def step(i, carry):
        ring_copy(i, *args).start()
        return carry

    lax.fori_loop(1, args[-1], step, 0)


def wait_arrived(*args):
    def step(i, carry):
        arrived_copy(i, *args).wait_recv()
        return carry

    lax.fori_loop(1, args[-1], step, 0)


def wait_sent(*args):
    def step(i, carry):
        ring_copy(i, *args).wait_send()
        return carry

    lax.fori_loop(1, args[-1], step, 0)


def reduce_plans(packed, land_a, part, land_b, result, sems):
    a_send, a_receive, b_send, b_receive, c_send, c_receive = sems
    first = (lambda me, peer: packed.at[pl.ds(4 * peer, 4)], lambda me, peer: land_a.at[me], a_send, a_receive, 8)
    second = (lambda me, peer: part, lambda me, peer: land_b.at[me], b_send, b_receive, 16)
    third = (lambda me, peer: land_b.at[16], lambda me, peer: result.at[pl.ds(4 * me, 4)], c_send, c_receive, 8)
    return first, second, third


def reduce_first(plans, packed, land_a, part, land_b):
    d, t, chip, core = place()
    me = d * 2 + core
    wait_arrived(*plans[0])
    land_a[me] = packed[pl.ds(4 * me, 4)]
    total = land_a[0]
    for j in range(1, 8):
        total += land_a[j]
    part[...] = total
    land_b[t // 2] = total
    start_all(*plans[1])


def reduce_second(plans, part, land_b, result, factor):
    d, t, chip, core = place()
    me = d * 2 + core
    wait_arrived(*plans[1])
    total = land_b[0]
    for j in range(1, 16):
        total += land_b[j]
    total = total * factor
    land_b[16] = total
    result[pl.ds(4 * me, 4)] = total
    start_all(*plans[2])


def unpack_gradient(result, out, w):
    for r in range(27):
        tile = result[r]
        for g in range(4):
            t = 27 * g + r
            moved = tile if g == 0 else pltpu.roll(tile, 128 - 32 * g, 1)
            out[w, t // 4, pl.ds(8 * (t % 4), 8), :] = moved[:, :32]


def kernel(
    features_in, cotangent_in, first_in, second_in, links_in, depth_in, tile_in, workers_in,
    moved, gradients_out,
    features, cotangent, first_weight, second_weight, links, send_depth, send_tile, workers, gradients,
    table_x, table_g, even_x, odd_x, even_g, odd_g, wide_first, wide_second, pre, back, hidden, folded,
    grad_pre, grad_input, outgoing,
    stage_d, land_d, stage_t, land_t, sections,
    stage_d2, land_d2, stage_t2, land_t2, sections2,
    packed, land_a, part, land_b, result,
    d_send, d_receive, t_send, t_receive, d2_send, d2_receive, t2_send, t2_receive,
    load_sem, store_sem, m_send, m_receive, own_sem, a_send, a_receive, b_send, b_receive, c_send, c_receive,
):
    d, t, chip, core = place()
    fields, tables = (features, cotangent), (table_x, table_g)
    pairs = (
        (features_in, features), (cotangent_in, cotangent), (depth_in, send_depth), (tile_in, send_tile),
        (links_in, links), (workers_in, workers), (first_in, first_weight), (second_in, second_weight),
    )
    loads = [pltpu.make_async_copy(source, target, load_sem.at[i]) for i, (source, target) in enumerate(pairs)]
    for load in loads:
        load.start()
    barrier = greet()
    for load in loads:
        load.wait()
    stage_depth(fields, send_depth, stage_d)
    pl.semaphore_wait(barrier, TILES - 1 + 2 * (DEPTHS - 1))
    along_depth = depth_copies(stage_d, land_d, d_send, d_receive)
    for copy in along_depth:
        copy.start()
    table_own(fields, tables)
    table_x[16] = jnp.zeros((64, 8, 128), F32)
    table_g[16] = jnp.zeros((64, 8, 128), F32)
    spread_weight(first_weight, wide_first)
    for copy in along_depth:
        copy.wait()
    accept_depth(fields, land_d, sections, tables)
    stage_tile(2, sections, send_tile, stage_t)
    along_tile = tile_copies(stage_t, land_t, t_send, t_receive)
    for copy in along_tile:
        copy.start()
    table_depth(sections, tables)
    spread_weight(second_weight, wide_second)
    for copy in along_tile:
        copy.wait()
    table_tile(land_t, tables)
    build_shifts(table_x, links, even_x, odd_x)
    build_shifts(table_g, links, even_g, odd_g)
    pre[...] = jnp.zeros((512, 256), F32)
    back[...] = jnp.zeros((512, 256), F32)
    conv_forward(even_x, odd_x, wide_first, pre)
    conv_backward(even_g, odd_g, wide_second, back)
    value = pre[...]
    sigma = 1.0 / (1.0 + jnp.exp(-value))
    hidden[...] = (value * sigma).T.astype(BF16)
    grad_pre[...] = (back[...] * sigma * (1.0 + value * (1.0 - sigma))).T.astype(BF16).reshape(8, 32, 512)

    stage_depth((grad_pre,), send_depth, stage_d2)
    along_depth = depth_copies(stage_d2, land_d2, d2_send, d2_receive)
    for copy in along_depth:
        copy.start()
    weight_gradient(lambda: hidden[...], even_g, odd_g, folded)
    for copy in along_depth:
        copy.wait()
    accept_depth((grad_pre,), land_d2, sections2, tables)
    stage_tile(1, sections2, send_tile, stage_t2)
    along_tile = tile_copies(stage_t2, land_t2, t2_send, t2_receive)
    for copy in along_tile:
        copy.start()
    pack_gradient(folded, packed.at[1])
    plans = [
        reduce_plans(
            packed.at[w], land_a.at[w], part.at[w], land_b.at[w], result.at[w],
            tuple(s.at[w] for s in (a_send, a_receive, b_send, b_receive, c_send, c_receive)),
        )
        for w in range(2)
    ]
    start_all(*plans[1][0])
    table_own((grad_pre,), tables[:1])
    table_depth(sections2, tables[:1])
    for copy in along_tile:
        copy.wait()
    table_tile(land_t2, tables[:1])
    build_shifts(table_x, links, even_x, odd_x)
    back[...] = jnp.zeros((512, 256), F32)
    conv_backward(even_x, odd_x, wide_first, back)
    reduce_first(plans[1], packed.at[1], land_a.at[1], part.at[1], land_b.at[1])
    grad_input[0:8] = (back[...].T.reshape(8, 32, 512) + cotangent[...].astype(F32)).astype(BF16)
    grad_input[8] = jnp.zeros((32, 512), BF16)

    names = [workers[0, n] for n in range(8)]
    slots = []
    for n in range(8):
        rank = jnp.int32(0)
        for m in range(n):
            rank = rank + jnp.where(names[m] == names[n], 1, 0)
        slots.append(2 * names[n] + rank)

    def place_brick(s, carry):
        brick = jnp.int32(8)
        for n in range(8):
            brick = jnp.where(slots[n] == s, n, brick)
        outgoing[s] = grad_input[brick]
        return carry

    lax.fori_loop(0, 2 * TILES, place_brick, 0)
    own = pltpu.make_async_copy(outgoing.at[pl.ds(2 * t, 2)], moved.at[pl.ds(2 * t, 2)], own_sem)
    own.start()
    factor = float(DEPTHS * TILES * 8 * 512) ** (-0.5)
    for i in range(0, 10):
        move(i, outgoing, moved, m_send, m_receive).start()
    weight_gradient(lambda: features[...].reshape(256, 512), even_x, odd_x, folded)
    pack_gradient(folded, packed.at[0])
    start_all(*plans[0][0])
    for i in range(10, 17):
        move(i, outgoing, moved, m_send, m_receive).start()
    reduce_second(plans[1], part.at[1], land_b.at[1], result.at[1], factor)
    reduce_first(plans[0], packed.at[0], land_a.at[0], part.at[0], land_b.at[0])
    for i in range(17, 24):
        move(i, outgoing, moved, m_send, m_receive).start()
    wait_arrived(*plans[1][2])
    unpack_gradient(result.at[1], gradients, 1)
    reduce_second(plans[0], part.at[0], land_b.at[0], result.at[0], factor)
    for i in range(24, 31):
        move(i, outgoing, moved, m_send, m_receive).start()
    wait_arrived(*plans[0][2])
    unpack_gradient(result.at[0], gradients, 0)
    store = pltpu.make_async_copy(gradients, gradients_out, store_sem)
    store.start()
    for w in range(2):
        for plan in plans[w]:
            wait_sent(*plan)
    own.wait()
    for i in range(31):
        landed(i, outgoing, moved, m_send, m_receive).wait_recv()
        move(i, outgoing, moved, m_send, m_receive).wait_send()
    store.wait()


def hand_over(moved_in, gradients_in, moved, gradients, held, held_gradients, in_sems, out_sems):
    spans = [(moved_in, held, moved, pl.ds(8 * i, 8)) for i in range(8)]
    spans += [(gradients_in, held_gradients, gradients, pl.ds(i, 1)) for i in range(2)]
    loads = [pltpu.make_async_copy(a.at[at], b.at[at], in_sems.at[i]) for i, (a, b, c, at) in enumerate(spans)]
    stores = [pltpu.make_async_copy(b.at[at], c.at[at], out_sems.at[i]) for i, (a, b, c, at) in enumerate(spans)]
    for load in loads:
        load.start()
    for load, store in zip(loads, stores):
        load.wait()
        store.start()
    for store in stores:
        store.wait()


def local(features, cotangent, first_weight, second_weight, neighbours, send_depth, send_tile, worker_tile):
    anywhere = pl.BlockSpec(memory_space=pl.ANY)
    brick = (32, 512)
    shifts = [pltpu.VMEM((3, 10, 80, 256), BF16), pltpu.VMEM((3, 10, 64, 256), BF16)]

    def halo(count):
        return [pltpu.VMEM((2, 2 * count, *brick), BF16)] * 4 + [pltpu.VMEM((count, 12, *brick), BF16)]

    dma = pltpu.SemaphoreType.DMA
    results = pl.pallas_call(
        kernel,
        out_shape=(
            jax.ShapeDtypeStruct((2 * TILES, *brick), BF16),
            jax.ShapeDtypeStruct((2, 27, 32, 32), F32),
        ),
        in_specs=[anywhere] * 8,
        out_specs=(anywhere, anywhere),
        scratch_shapes=[pltpu.VMEM((8, *brick), BF16)] * 2
        + [pltpu.VMEM((27, 32, 32), BF16)] * 2
        + [pltpu.SMEM((8, 26), jnp.int32), pltpu.SMEM((1, 2, 2), jnp.int32), pltpu.SMEM((1, 2, 2), jnp.int32), pltpu.SMEM((1, 8), jnp.int32)]
        + [pltpu.VMEM((2, 27, 32, 32), F32)]
        + [pltpu.VMEM((17, 64, 8, 128), F32)] * 2
        + shifts * 2
        + [pltpu.VMEM((3, 2304, 256), BF16)] * 2
        + [pltpu.VMEM((512, 256), F32)] * 2
        + [pltpu.VMEM((256, 512), BF16), pltpu.VMEM((864, 128), F32)]
        + [pltpu.VMEM((8, *brick), BF16), pltpu.VMEM((9, *brick), BF16), pltpu.VMEM((64, *brick), BF16)]
        + halo(2)
        + halo(1)
        + [
            pltpu.VMEM((2, 32, 8, 128), F32),
            pltpu.VMEM((2, 8, 4, 8, 128), F32),
            pltpu.VMEM((2, 4, 8, 128), F32),
            pltpu.VMEM((2, 17, 4, 8, 128), F32),
            pltpu.VMEM((2, 32, 8, 128), F32),
        ]
        + [dma((2,))] * 8
        + [dma((8,)), dma]
        + [dma((TILES - 1,))] * 2
        + [dma]
        + [dma((2, 8))] * 2
        + [dma((2, 16))] * 2
        + [dma((2, 8))] * 2,
        compiler_params=pltpu.CompilerParams(
            collective_id=0, has_side_effects=True, vmem_limit_bytes=64 * 2**20 - 2**17
        ),
    )(features, cotangent, first_weight, second_weight, neighbours, send_depth, send_tile, worker_tile.reshape(1, 8))
    return pl.pallas_call(
        hand_over,
        out_shape=tuple(jax.ShapeDtypeStruct(r.shape, r.dtype) for r in results),
        in_specs=[anywhere] * 2,
        out_specs=(anywhere, anywhere),
        scratch_shapes=[pltpu.VMEM((2 * TILES, *brick), BF16), pltpu.VMEM((2, 27, 32, 32), F32), dma((10,)), dma((10,))],
        compiler_params=pltpu.CompilerParams(vmem_limit_bytes=64 * 2**20 - 2**17),
    )(*results)


def solution(mesh):
    rows = P(("depth", "tile"))
    placed = (rows, rows, P(), P(), rows, rows, rows, rows)
    return jax.shard_map(local, mesh=mesh, in_specs=placed, out_specs=(rows, P()), check_vma=False)
```

```python
import jax
import jax.numpy as jnp
from jax import lax
from jax.experimental import pallas as pl
from jax.experimental.pallas import tpu as pltpu
from jax.sharding import PartitionSpec as P

F32 = jnp.float32
BF16 = jnp.bfloat16


def iota(shape, dim):
    return lax.broadcasted_iota(jnp.int32, shape, dim)


def tiled_identity(lanes):
    return jnp.where(iota((32, lanes), 1) % 32 == iota((32, lanes), 0), 1.0, 0.0).astype(BF16)


def fill_table(table, slot, brick):
    spread = lax.dot_general(brick, tiled_identity(128), (((0,), (0,)), ((), ())), preferred_element_type=F32)
    table[slot] = spread.reshape(64, 8, 128)


def spread_weight(weight, wide):
    columns = iota((32, 256), 1) // 32
    rows = jnp.dot(weight[...].reshape(864, 32), tiled_identity(256), preferred_element_type=F32).astype(BF16)
    for k in range(27):
        for n in range(8):
            part = jnp.where(columns == n, rows[32 * k : 32 * k + 32], jnp.zeros((), BF16))
            wide[k // 9, pl.ds(256 * (k % 9) + 32 * n, 32), :] = part


def build_shifts(table, links, even, odd):
    lane = iota((8, 128), 1)
    sub = iota((8, 128), 0)

    def one_plane(a_block, a_source, a_row):
        entry = {}
        for rest in range(9):
            k = a_block * 9 + rest
            for n in range(8):
                if k == 13:
                    entry[rest, n] = n
                else:
                    link = links[n, k - (k > 13)]
                    entry[rest, n] = jnp.where(link < 0, 16, link)

        for half in range(2):
            def mixed(rest, b_source):
                parts = [table[entry[rest, 4 * half + j], a_source * 8 + b_source] for j in range(4)]
                low = jnp.where(lane < 32, parts[0], parts[1])
                high = jnp.where(lane < 96, parts[2], parts[3])
                return jnp.where(lane < 64, low, high)

            columns = pl.ds(128 * half, 128)
            rows = []
            for b in range(10):
                b_block, b_source = (b + 7) // 8, (b + 7) % 8
                mid = mixed(b_block * 3 + 1, b_source)
                lower = mixed(b_block * 3, b_source)
                upper = mixed(b_block * 3 + 2, b_source)
                down = pltpu.roll(jnp.where(sub == 7, lower, mid), 1, 0)
                up = pltpu.roll(jnp.where(sub == 0, upper, mid), 7, 0)
                rows.append((down, mid, up))
                if b > 0:
                    for v in range(3):
                        pair = jnp.concatenate([rows[b - 1][v], rows[b][v]], 0).astype(BF16)
                        if b % 2:
                            even[v, a_row, pl.ds(8 * (b - 1), 16), columns] = pair
                        else:
                            odd[v, a_row, pl.ds(8 * (b - 2), 16), columns] = pair

    one_plane(0, 7, 0)

    def middle(a, carry):
        one_plane(1, a, a + 1)
        return carry

    lax.fori_loop(0, 8, middle, 0)
    one_plane(2, 0, 9)


def piece(even, odd, a, rest):
    b, c = rest // 3, rest % 3
    source = odd[c, pl.ds(a, 8)] if b == 1 else even[c, pl.ds(a, 8), pl.ds(8 * b, 64)]
    return source.reshape(512, 256)


def conv_forward(even, odd, wide, total):
    def step(a, carry):
        left = jnp.concatenate([piece(even, odd, a, rest) for rest in range(9)], 1)
        total[...] += jnp.dot(left, wide[a], preferred_element_type=F32)
        return carry

    lax.fori_loop(0, 3, step, 0)


def conv_backward(even, odd, wide, total):
    def step(a, carry):
        acc = total[...]
        for rest in range(9):
            acc += lax.dot_general(
                piece(even, odd, a, rest), wide[2 - a, pl.ds(256 * (8 - rest), 256), :], (((1,), (1,)), ((), ())), preferred_element_type=F32
            )
        total[...] = acc
        return carry

    lax.fori_loop(0, 3, step, 0)


def weight_gradient(left_of, even, odd, folded):
    lane = iota((32, 128), 1)

    def step(a, carry):
        for rest in range(9):
            full = jnp.dot(left_of(), piece(even, odd, a, rest), preferred_element_type=F32)
            halves = []
            for half in range(2):
                parts = [full[128 * half + 32 * j : 128 * half + 32 * j + 32, 128 * half : 128 * half + 128] for j in range(4)]
                low = jnp.where(lane < 32, parts[0], parts[1])
                high = jnp.where(lane < 96, parts[2], parts[3])
                halves.append(jnp.where(lane < 64, low, high))
            both = halves[0] + halves[1]
            both = both + pltpu.roll(both, 64, 1)
            both = both + pltpu.roll(both, 32, 1)
            folded[pl.ds(pl.multiple_of(32 * (9 * (2 - a) + 8 - rest), 32), 32), :] = both
        return carry

    lax.fori_loop(0, 3, step, 0)


def pack_gradient(folded, packed):
    lane = iota((8, 128), 1)
    for r in range(27):
        parts = [folded[pl.ds(8 * (27 * g + r), 8), :] for g in range(4)]
        low = jnp.where(lane < 32, parts[0], parts[1])
        high = jnp.where(lane < 96, parts[2], parts[3])
        packed[r] = jnp.where(lane < 64, low, high)
    packed[27:32] = jnp.zeros((5, 8, 128), F32)

MESH = pl.DeviceIdType.MESH
DEPTHS, TILES = 4, 32


def remote(source, target, send, receive, device):
    return pltpu.make_async_remote_copy(
        src_ref=source, dst_ref=target, send_sem=send, recv_sem=receive, device_id=device, device_id_type=MESH
    )


def place():
    d, t = lax.axis_index("depth"), lax.axis_index("tile")
    return d, t, (t // 2) * 2, t % 2


def flipped(value, bit):
    step = 2**bit
    return value + step - 2 * step * ((value // step) % 2)


def greet():
    d, t, chip, core = place()
    barrier = pltpu.get_barrier_semaphore()
    peers = [(d, flipped(t, bit)) for bit in range(5)]
    peers += [(d, (t + 1) % TILES), (d, (t + TILES - 1) % TILES)]
    peers += [((d + step) % DEPTHS, t) for step in range(1, DEPTHS)]
    for peer in peers:
        pl.semaphore_signal(barrier, inc=1, device_id=peer, device_id_type=MESH)
    return barrier, len(peers)


def spread_word(round_sem, step):
    d, t, _, _ = place()
    if step > 0:
        pl.semaphore_wait(round_sem.at[step - 1], 1)
    if step < 6:
        peer = (d, flipped(t, step + 1)) if step < 4 else (flipped(d, step - 4), t)
        pl.semaphore_signal(round_sem.at[step], inc=1, device_id=peer, device_id_type=MESH)


def depth_copies(stage, land, sends, receives):
    d, t, _, _ = place()
    return (
        remote(stage.at[0], land.at[1], sends.at[0], receives.at[1], ((d + DEPTHS - 1) % DEPTHS, t)),
        remote(stage.at[1], land.at[0], sends.at[1], receives.at[0], ((d + 1) % DEPTHS, t)),
    )


def tile_copies(stage, land, sends, receives):
    d, t, _, _ = place()
    return (
        remote(stage.at[0], land.at[1], sends.at[0], receives.at[1], (d, (t + TILES - 1) % TILES)),
        remote(stage.at[1], land.at[0], sends.at[1], receives.at[0], (d, (t + 1) % TILES)),
    )


def stage_depth(fields, send_depth, stage):
    for side in range(2):
        for f, field in enumerate(fields):
            for j in range(2):
                stage[side, 2 * f + j] = field[send_depth[0, side, j]]


def accept_depth(fields, land, sections, tables):
    d, _, _, _ = place()
    inner = (d > 0, d < DEPTHS - 1)
    for f, field in enumerate(fields):
        sections[f, 0:8] = field[...]
        for side in range(2):
            for j in range(2):
                value = land[side, 2 * f + j]
                value = jnp.where(inner[side], value, jnp.zeros_like(value))
                sections[f, 8 + 2 * side + j] = value


def stage_tile(count, sections, send_tile, stage):
    for side in range(2):
        for f in range(count):
            for j in range(2):
                stage[side, 2 * f + j] = sections[f, send_tile[0, side, j]]


def table_own(fields, tables):
    for field, table in zip(fields, tables):
        for m in range(8):
            fill_table(table, m, field[m])


def table_depth(sections, tables):
    for f, table in enumerate(tables):
        for j in range(4):
            fill_table(table, 8 + j, sections[f, 8 + j])


def table_tile(land, tables):
    for f, table in enumerate(tables):
        for side in range(2):
            for j in range(2):
                fill_table(table, 12 + 2 * side + j, land[side, 2 * f + j])


ORDER = (
    (1, 2, 1), (3, 1, 0), (0, 3, 1), (2, 2, 0), (0, 0, 1), (1, 3, 0),
    (3, 1, 1), (1, 0, 0), (2, 2, 1), (0, 1, 0), (1, 3, 1), (3, 2, 0),
    (1, 0, 1), (2, 3, 0), (0, 1, 1), (2, 0, 0), (3, 2, 1), (1, 1, 0),
    (2, 3, 1), (0, 2, 0), (2, 0, 1), (3, 3, 0), (1, 1, 1), (3, 0, 0),
    (0, 2, 1), (2, 1, 0), (3, 3, 1), (1, 2, 0), (3, 0, 1), (0, 3, 0),
    (2, 1, 1),
)


def shifted_tile(i):
    t = lax.axis_index("tile")
    dy, dx, dc = ORDER[i]
    y, x, core = t // 8, (t // 2) % 4, t % 2
    return ((y + dy) % 4) * 8 + ((x + dx) % 4) * 2 + (core + dc) % 2


def move(i, outgoing, moved, sends, receives):
    d, t = lax.axis_index("depth"), lax.axis_index("tile")
    peer = shifted_tile(i)
    return remote(outgoing.at[pl.ds(2 * peer, 2)], moved.at[pl.ds(2 * t, 2)], sends, receives, (d, peer))


def ring_copy(i, plan):
    source, target, _, send, receive, group = plan
    d, t, chip, core = place()
    if group == 8:
        me = d * 2 + core
        peer = (me + i) % 8
        device = (peer // 2, chip + peer % 2)
    else:
        me = t // 2
        peer = (me + i) % 16
        device = (d, 2 * peer + core)
    return remote(source(me, peer), target(me, peer), send, receive, device)


def start_all(plan):
    def step(i, carry):
        ring_copy(i, plan).start()
        return carry

    lax.fori_loop(1, plan[-1], step, 0)


def all_of(whole, send, receive):
    d, t, _, _ = place()
    return remote(whole, whole, send, receive, (d, (t + 1) % TILES))


def wait_arrived(plan):
    all_of(plan[2], plan[3], plan[4]).wait_recv()


def wait_sent(plan):
    all_of(plan[2], plan[3], plan[4]).wait_send()


def reduce_plans(packed, land_a, part, land_b, result, sems):
    a_send, a_receive, b_send, b_receive, c_send, c_receive = sems
    first = (
        lambda me, peer: packed.at[pl.ds(4 * peer, 4)], lambda me, peer: land_a.at[me], land_a.at[pl.ds(0, 7)],
        a_send, a_receive, 8,
    )
    second = (lambda me, peer: part, lambda me, peer: land_b.at[me], land_b.at[pl.ds(0, 15)], b_send, b_receive, 16)
    third = (
        lambda me, peer: land_b.at[16], lambda me, peer: result.at[pl.ds(4 * me, 4)], result.at[pl.ds(0, 28)],
        c_send, c_receive, 8,
    )
    return first, second, third


def reduce_first(plans, packed, land_a, part, land_b):
    d, t, chip, core = place()
    me = d * 2 + core
    wait_arrived(plans[0])
    land_a[me] = packed[pl.ds(4 * me, 4)]
    total = land_a[0]
    for j in range(1, 8):
        total += land_a[j]
    part[...] = total
    land_b[t // 2] = total
    start_all(plans[1])


def reduce_second(plans, part, land_b, result, factor):
    d, t, chip, core = place()
    me = d * 2 + core
    wait_arrived(plans[1])
    total = land_b[0]
    for j in range(1, 16):
        total += land_b[j]
    total = total * factor
    land_b[16] = total
    result[pl.ds(4 * me, 4)] = total
    start_all(plans[2])


def unpack_gradient(result, out, w):
    for r in range(27):
        tile = result[r]
        for g in range(4):
            t = 27 * g + r
            moved = tile if g == 0 else pltpu.roll(tile, 128 - 32 * g, 1)
            out[w, t // 4, pl.ds(8 * (t % 4), 8), :] = moved[:, :32]


def kernel(
    features_in, cotangent_in, first_in, second_in, links_in, depth_in, tile_in, workers_in,
    moved, gradients_out,
    features, cotangent, first_weight, second_weight, links, send_depth, send_tile, workers, gradients,
    table_x, table_g, even_x, odd_x, even_g, odd_g, wide_first, wide_second, pre, back, hidden, folded,
    grad_pre, grad_input, outgoing,
    stage_d, land_d, stage_t, land_t, sections,
    stage_d2, land_d2, stage_t2, land_t2, sections2,
    packed, land_a, part, land_b, result,
    d_send, d_receive, t_send, t_receive, d2_send, d2_receive, t2_send, t2_receive,
    load_sem, store_sem, m_send, m_receive, own_sem, a_send, a_receive, b_send, b_receive, c_send, c_receive, round_sem,
):
    d, t, chip, core = place()
    fields, tables = (features, cotangent), (table_x, table_g)
    pairs = (
        (features_in, features), (cotangent_in, cotangent), (depth_in, send_depth), (tile_in, send_tile),
        (links_in, links), (workers_in, workers), (first_in, first_weight), (second_in, second_weight),
    )
    loads = [pltpu.make_async_copy(source, target, load_sem.at[i]) for i, (source, target) in enumerate(pairs)]
    for load in loads:
        load.start()
    barrier, greetings = greet()
    for load in loads:
        load.wait()
    stage_depth(fields, send_depth, stage_d)
    pl.semaphore_wait(barrier, greetings)
    along_depth = depth_copies(stage_d, land_d, d_send, d_receive)
    for copy in along_depth:
        copy.start()
    table_own(fields, tables)
    table_x[16] = jnp.zeros((64, 8, 128), F32)
    table_g[16] = jnp.zeros((64, 8, 128), F32)
    spread_weight(first_weight, wide_first)
    spread_word(round_sem, 0)
    for copy in along_depth:
        copy.wait()
    accept_depth(fields, land_d, sections, tables)
    stage_tile(2, sections, send_tile, stage_t)
    along_tile = tile_copies(stage_t, land_t, t_send, t_receive)
    for copy in along_tile:
        copy.start()
    table_depth(sections, tables)
    spread_weight(second_weight, wide_second)
    spread_word(round_sem, 1)
    for copy in along_tile:
        copy.wait()
    table_tile(land_t, tables)
    build_shifts(table_x, links, even_x, odd_x)
    spread_word(round_sem, 2)
    build_shifts(table_g, links, even_g, odd_g)
    spread_word(round_sem, 3)
    pre[...] = jnp.zeros((512, 256), F32)
    back[...] = jnp.zeros((512, 256), F32)
    conv_forward(even_x, odd_x, wide_first, pre)
    spread_word(round_sem, 4)
    conv_backward(even_g, odd_g, wide_second, back)
    spread_word(round_sem, 5)
    value = pre[...]
    sigma = 1.0 / (1.0 + jnp.exp(-value))
    hidden[...] = (value * sigma).T.astype(BF16)
    grad_pre[...] = (back[...] * sigma * (1.0 + value * (1.0 - sigma))).T.astype(BF16).reshape(8, 32, 512)

    stage_depth((grad_pre,), send_depth, stage_d2)
    along_depth = depth_copies(stage_d2, land_d2, d2_send, d2_receive)
    for copy in along_depth:
        copy.start()
    weight_gradient(lambda: hidden[...], even_g, odd_g, folded)
    spread_word(round_sem, 6)
    for copy in along_depth:
        copy.wait()
    accept_depth((grad_pre,), land_d2, sections2, tables)
    stage_tile(1, sections2, send_tile, stage_t2)
    along_tile = tile_copies(stage_t2, land_t2, t2_send, t2_receive)
    for copy in along_tile:
        copy.start()
    pack_gradient(folded, packed.at[1])
    plans = [
        reduce_plans(
            packed.at[w], land_a.at[w], part.at[w], land_b.at[w], result.at[w],
            tuple(s.at[w] for s in (a_send, a_receive, b_send, b_receive, c_send, c_receive)),
        )
        for w in range(2)
    ]
    start_all(plans[1][0])
    table_own((grad_pre,), tables[:1])
    table_depth(sections2, tables[:1])
    for copy in along_tile:
        copy.wait()
    table_tile(land_t2, tables[:1])
    build_shifts(table_x, links, even_x, odd_x)
    back[...] = jnp.zeros((512, 256), F32)
    conv_backward(even_x, odd_x, wide_first, back)
    reduce_first(plans[1], packed.at[1], land_a.at[1], part.at[1], land_b.at[1])
    grad_input[0:8] = (back[...].T.reshape(8, 32, 512) + cotangent[...].astype(F32)).astype(BF16)
    grad_input[8] = jnp.zeros((32, 512), BF16)

    names = [workers[0, n] for n in range(8)]
    slots = []
    for n in range(8):
        rank = jnp.int32(0)
        for m in range(n):
            rank = rank + jnp.where(names[m] == names[n], 1, 0)
        slots.append(2 * names[n] + rank)

    def place_brick(s, carry):
        brick = jnp.int32(8)
        for n in range(8):
            brick = jnp.where(slots[n] == s, n, brick)
        outgoing[s] = grad_input[brick]
        return carry

    lax.fori_loop(0, 2 * TILES, place_brick, 0)
    own = pltpu.make_async_copy(outgoing.at[pl.ds(2 * t, 2)], moved.at[pl.ds(2 * t, 2)], own_sem)
    own.start()
    factor = float(DEPTHS * TILES * 8 * 512) ** (-0.5)
    for i in range(0, 10):
        move(i, outgoing, moved, m_send, m_receive).start()
    weight_gradient(lambda: features[...].reshape(256, 512), even_x, odd_x, folded)
    pack_gradient(folded, packed.at[0])
    start_all(plans[0][0])
    for i in range(10, 17):
        move(i, outgoing, moved, m_send, m_receive).start()
    reduce_second(plans[1], part.at[1], land_b.at[1], result.at[1], factor)
    reduce_first(plans[0], packed.at[0], land_a.at[0], part.at[0], land_b.at[0])
    for i in range(17, 24):
        move(i, outgoing, moved, m_send, m_receive).start()
    wait_arrived(plans[1][2])
    unpack_gradient(result.at[1], gradients, 1)
    reduce_second(plans[0], part.at[0], land_b.at[0], result.at[0], factor)
    for i in range(24, 31):
        move(i, outgoing, moved, m_send, m_receive).start()
    wait_arrived(plans[0][2])
    unpack_gradient(result.at[0], gradients, 0)
    store = pltpu.make_async_copy(gradients, gradients_out, store_sem)
    store.start()
    for w in range(2):
        for plan in plans[w]:
            wait_sent(plan)
    own.wait()
    whole = all_of(moved.at[pl.ds(0, 62)], m_send, m_receive)
    whole.wait_recv()
    whole.wait_send()
    store.wait()


def hand_over(moved_in, gradients_in, moved, gradients, held, held_gradients, in_sems, out_sems):
    spans = [(moved_in, held, moved, pl.ds(8 * i, 8)) for i in range(8)]
    spans += [(gradients_in, held_gradients, gradients, pl.ds(i, 1)) for i in range(2)]
    loads = [pltpu.make_async_copy(a.at[at], b.at[at], in_sems.at[i]) for i, (a, b, c, at) in enumerate(spans)]
    stores = [pltpu.make_async_copy(b.at[at], c.at[at], out_sems.at[i]) for i, (a, b, c, at) in enumerate(spans)]
    for load in loads:
        load.start()
    for load, store in zip(loads, stores):
        load.wait()
        store.start()
    for store in stores:
        store.wait()


def local(features, cotangent, first_weight, second_weight, neighbours, send_depth, send_tile, worker_tile):
    anywhere = pl.BlockSpec(memory_space=pl.ANY)
    brick = (32, 512)
    shifts = [pltpu.VMEM((3, 10, 80, 256), BF16), pltpu.VMEM((3, 10, 64, 256), BF16)]

    def halo(count):
        return [pltpu.VMEM((2, 2 * count, *brick), BF16)] * 4 + [pltpu.VMEM((count, 12, *brick), BF16)]

    dma = pltpu.SemaphoreType.DMA
    results = pl.pallas_call(
        kernel,
        out_shape=(
            jax.ShapeDtypeStruct((2 * TILES, *brick), BF16),
            jax.ShapeDtypeStruct((2, 27, 32, 32), F32),
        ),
        in_specs=[anywhere] * 8,
        out_specs=(anywhere, anywhere),
        scratch_shapes=[pltpu.VMEM((8, *brick), BF16)] * 2
        + [pltpu.VMEM((27, 32, 32), BF16)] * 2
        + [pltpu.SMEM((8, 26), jnp.int32), pltpu.SMEM((1, 2, 2), jnp.int32), pltpu.SMEM((1, 2, 2), jnp.int32), pltpu.SMEM((1, 8), jnp.int32)]
        + [pltpu.VMEM((2, 27, 32, 32), F32)]
        + [pltpu.VMEM((17, 64, 8, 128), F32)] * 2
        + shifts * 2
        + [pltpu.VMEM((3, 2304, 256), BF16)] * 2
        + [pltpu.VMEM((512, 256), F32)] * 2
        + [pltpu.VMEM((256, 512), BF16), pltpu.VMEM((864, 128), F32)]
        + [pltpu.VMEM((8, *brick), BF16), pltpu.VMEM((9, *brick), BF16), pltpu.VMEM((64, *brick), BF16)]
        + halo(2)
        + halo(1)
        + [
            pltpu.VMEM((2, 32, 8, 128), F32),
            pltpu.VMEM((2, 8, 4, 8, 128), F32),
            pltpu.VMEM((2, 4, 8, 128), F32),
            pltpu.VMEM((2, 17, 4, 8, 128), F32),
            pltpu.VMEM((2, 32, 8, 128), F32),
        ]
        + [dma((2,))] * 8
        + [dma((8,)), dma]
        + [dma] * 3
        + [dma((2,))] * 6
        + [pltpu.SemaphoreType.REGULAR((6,))],
        compiler_params=pltpu.CompilerParams(
            collective_id=0, has_side_effects=True, vmem_limit_bytes=64 * 2**20 - 2**17
        ),
    )(features, cotangent, first_weight, second_weight, neighbours, send_depth, send_tile, worker_tile.reshape(1, 8))
    return pl.pallas_call(
        hand_over,
        out_shape=tuple(jax.ShapeDtypeStruct(r.shape, r.dtype) for r in results),
        in_specs=[anywhere] * 2,
        out_specs=(anywhere, anywhere),
        scratch_shapes=[pltpu.VMEM((2 * TILES, *brick), BF16), pltpu.VMEM((2, 27, 32, 32), F32), dma((10,)), dma((10,))],
        compiler_params=pltpu.CompilerParams(vmem_limit_bytes=64 * 2**20 - 2**17),
    )(*results)


def solution(mesh):
    rows = P(("depth", "tile"))
    placed = (rows, rows, P(), P(), rows, rows, rows, rows)
    return jax.shard_map(local, mesh=mesh, in_specs=placed, out_specs=(rows, P()), check_vma=False)
```

```python
import jax
import jax.numpy as jnp
from jax import lax
from jax.experimental import pallas as pl
from jax.experimental.pallas import tpu as pltpu
from jax.sharding import PartitionSpec as P

F32 = jnp.float32
BF16 = jnp.bfloat16


def iota(shape, dim):
    return lax.broadcasted_iota(jnp.int32, shape, dim)


def tiled_identity(lanes):
    return jnp.where(iota((32, lanes), 1) % 32 == iota((32, lanes), 0), 1.0, 0.0).astype(BF16)


def fill_table(table, slot, brick):
    spread = lax.dot_general(brick, tiled_identity(128), (((0,), (0,)), ((), ())), preferred_element_type=F32)
    table[slot] = spread.reshape(64, 8, 128)


def spread_weight(weight, wide):
    columns = iota((32, 256), 1) // 32
    rows = jnp.dot(weight[...].reshape(864, 32), tiled_identity(256), preferred_element_type=F32).astype(BF16)
    for k in range(27):
        for n in range(8):
            part = jnp.where(columns == n, rows[32 * k : 32 * k + 32], jnp.zeros((), BF16))
            wide[k // 9, pl.ds(256 * (k % 9) + 32 * n, 32), :] = part


def build_shifts(table, links, even, odd):
    lane = iota((8, 128), 1)
    sub = iota((8, 128), 0)

    def one_plane(a_block, a_source, a_row):
        entry = {}
        for rest in range(9):
            k = a_block * 9 + rest
            for n in range(8):
                if k == 13:
                    entry[rest, n] = n
                else:
                    link = links[n, k - (k > 13)]
                    entry[rest, n] = jnp.where(link < 0, 16, link)

        for half in range(2):
            def mixed(rest, b_source):
                parts = [table[entry[rest, 4 * half + j], a_source * 8 + b_source] for j in range(4)]
                low = jnp.where(lane < 32, parts[0], parts[1])
                high = jnp.where(lane < 96, parts[2], parts[3])
                return jnp.where(lane < 64, low, high)

            columns = pl.ds(128 * half, 128)
            rows = []
            for b in range(10):
                b_block, b_source = (b + 7) // 8, (b + 7) % 8
                mid = mixed(b_block * 3 + 1, b_source)
                lower = mixed(b_block * 3, b_source)
                upper = mixed(b_block * 3 + 2, b_source)
                down = pltpu.roll(jnp.where(sub == 7, lower, mid), 1, 0)
                up = pltpu.roll(jnp.where(sub == 0, upper, mid), 7, 0)
                rows.append((down, mid, up))
                if b > 0:
                    for v in range(3):
                        pair = jnp.concatenate([rows[b - 1][v], rows[b][v]], 0).astype(BF16)
                        if b % 2:
                            even[v, a_row, pl.ds(8 * (b - 1), 16), columns] = pair
                        else:
                            odd[v, a_row, pl.ds(8 * (b - 2), 16), columns] = pair

    one_plane(0, 7, 0)

    def middle(a, carry):
        one_plane(1, a, a + 1)
        return carry

    lax.fori_loop(0, 8, middle, 0)
    one_plane(2, 0, 9)


def piece(even, odd, a, rest):
    b, c = rest // 3, rest % 3
    source = odd[c, pl.ds(a, 8)] if b == 1 else even[c, pl.ds(a, 8), pl.ds(8 * b, 64)]
    return source.reshape(512, 256)


def conv_forward(even, odd, wide, total):
    def step(a, carry):
        left = jnp.concatenate([piece(even, odd, a, rest) for rest in range(9)], 1)
        total[...] += jnp.dot(left, wide[a], preferred_element_type=F32)
        return carry

    lax.fori_loop(0, 3, step, 0)


def conv_backward(even, odd, wide, total):
    def step(a, carry):
        acc = total[...]
        for rest in range(9):
            acc += lax.dot_general(
                piece(even, odd, a, rest), wide[2 - a, pl.ds(256 * (8 - rest), 256), :], (((1,), (1,)), ((), ())), preferred_element_type=F32
            )
        total[...] = acc
        return carry

    lax.fori_loop(0, 3, step, 0)


def weight_gradient(left_of, even, odd, folded):
    lane = iota((32, 128), 1)

    def step(a, carry):
        for rest in range(9):
            full = jnp.dot(left_of(), piece(even, odd, a, rest), preferred_element_type=F32)
            halves = []
            for half in range(2):
                parts = [full[128 * half + 32 * j : 128 * half + 32 * j + 32, 128 * half : 128 * half + 128] for j in range(4)]
                low = jnp.where(lane < 32, parts[0], parts[1])
                high = jnp.where(lane < 96, parts[2], parts[3])
                halves.append(jnp.where(lane < 64, low, high))
            both = halves[0] + halves[1]
            both = both + pltpu.roll(both, 64, 1)
            both = both + pltpu.roll(both, 32, 1)
            folded[pl.ds(pl.multiple_of(32 * (9 * (2 - a) + 8 - rest), 32), 32), :] = both
        return carry

    lax.fori_loop(0, 3, step, 0)


def pack_gradient(folded, packed):
    lane = iota((8, 128), 1)
    for r in range(27):
        parts = [folded[pl.ds(8 * (27 * g + r), 8), :] for g in range(4)]
        low = jnp.where(lane < 32, parts[0], parts[1])
        high = jnp.where(lane < 96, parts[2], parts[3])
        packed[r] = jnp.where(lane < 64, low, high)
    packed[27:32] = jnp.zeros((5, 8, 128), F32)

MESH = pl.DeviceIdType.MESH
DEPTHS, TILES = 4, 32


def remote(source, target, send, receive, device):
    return pltpu.make_async_remote_copy(
        src_ref=source, dst_ref=target, send_sem=send, recv_sem=receive, device_id=device, device_id_type=MESH
    )


def place():
    d, t = lax.axis_index("depth"), lax.axis_index("tile")
    return d, t, (t // 2) * 2, t % 2


def flipped(value, bit):
    step = 2**bit
    return value + step - 2 * step * ((value // step) % 2)


def greet():
    d, t, chip, core = place()
    barrier = pltpu.get_barrier_semaphore()
    peers = [(d, flipped(t, bit)) for bit in range(5)]
    peers += [(d, (t + 1) % TILES), (d, (t + TILES - 1) % TILES)]
    peers += [((d + step) % DEPTHS, t) for step in range(1, DEPTHS)]
    for peer in peers:
        pl.semaphore_signal(barrier, inc=1, device_id=peer, device_id_type=MESH)
    return barrier, len(peers)


def spread_word(round_sem, step):
    d, t, _, _ = place()
    if step > 0:
        pl.semaphore_wait(round_sem.at[step - 1], 1)
    if step < 6:
        peer = (d, flipped(t, step + 1)) if step < 4 else (flipped(d, step - 4), t)
        pl.semaphore_signal(round_sem.at[step], inc=1, device_id=peer, device_id_type=MESH)


def depth_copies(stage, land, sends, receives):
    d, t, _, _ = place()
    return (
        remote(stage.at[0], land.at[1], sends.at[0], receives.at[1], ((d + DEPTHS - 1) % DEPTHS, t)),
        remote(stage.at[1], land.at[0], sends.at[1], receives.at[0], ((d + 1) % DEPTHS, t)),
    )


def tile_copies(stage, land, sends, receives):
    d, t, _, _ = place()
    return (
        remote(stage.at[0], land.at[1], sends.at[0], receives.at[1], (d, (t + TILES - 1) % TILES)),
        remote(stage.at[1], land.at[0], sends.at[1], receives.at[0], (d, (t + 1) % TILES)),
    )


def stage_depth(fields, send_depth, stage):
    for side in range(2):
        for f, field in enumerate(fields):
            for j in range(2):
                stage[side, 2 * f + j] = field[send_depth[0, side, j]]


def accept_depth(fields, land, sections, tables):
    d, _, _, _ = place()
    inner = (d > 0, d < DEPTHS - 1)
    for f, field in enumerate(fields):
        sections[f, 0:8] = field[...]
        for side in range(2):
            for j in range(2):
                value = land[side, 2 * f + j]
                value = jnp.where(inner[side], value, jnp.zeros_like(value))
                sections[f, 8 + 2 * side + j] = value


def stage_tile(count, sections, send_tile, stage):
    for side in range(2):
        for f in range(count):
            for j in range(2):
                stage[side, 2 * f + j] = sections[f, send_tile[0, side, j]]


def table_own(fields, tables):
    for field, table in zip(fields, tables):
        for m in range(8):
            fill_table(table, m, field[m])


def table_depth(sections, tables):
    for f, table in enumerate(tables):
        for j in range(4):
            fill_table(table, 8 + j, sections[f, 8 + j])


def table_tile(land, tables):
    for f, table in enumerate(tables):
        for side in range(2):
            for j in range(2):
                fill_table(table, 12 + 2 * side + j, land[side, 2 * f + j])


def line_tile(axis, step, turn=0):
    t = lax.axis_index("tile")
    y, x, core = t // 8, (t // 2) % 4, (t + turn) % 2
    if axis == 0:
        return y * 8 + ((x + step) % 4) * 2 + core
    return ((y + step) % 4) * 8 + x * 2 + core


def line_place(axis):
    t = lax.axis_index("tile")
    return (t // 2) % 4 if axis == 0 else t // 8


def share_workers(workers_in, names_land, sends, receives, own_sems):
    d = lax.axis_index("depth")
    remotes, owns = [], []
    for axis in range(2):
        slot = names_land.at[4 * axis + line_place(axis)]
        owns.append(pltpu.make_async_copy(workers_in, slot, own_sems.at[axis]))
        for step in (1, 2, 3):
            remotes.append(remote(workers_in, slot, sends, receives, (d, line_tile(axis, step))))
    return remotes, owns


def broadcast_copy(axis, step, grad_input, gather, sends, receives):
    d = lax.axis_index("depth")
    return remote(
        grad_input.at[pl.ds(0, 8), pl.ds(16 * axis, 16)],
        gather.at[axis, line_place(axis), pl.ds(0, 8)],
        sends.at[axis],
        receives.at[axis],
        (d, line_tile(axis, step)),
    )


def find_slots(names, slots):
    for line in range(8):
        own = [names[line, 0, n] for n in range(8)]
        for n in range(8):
            rank = jnp.int32(0)
            for m in range(n):
                rank = rank + jnp.where(own[m] == own[n], 1, 0)
            slots[line, n] = 2 * own[n] + rank


def fill_message(axis, index, target, gather, slots, outgoing):
    for source in range(4):
        held = [slots[4 * axis + source, n] for n in range(8)]
        for q in range(2):
            key = 2 * target + q
            brick = jnp.int32(8)
            for n in range(8):
                brick = jnp.where(held[n] == key, n, brick)
            outgoing[axis, index, source, q] = gather[axis, source, brick]


def message_target(axis, moved):
    t = lax.axis_index("tile")
    y, x, core = t // 8, (t // 2) % 4, t % 2
    if axis == 0:
        return moved.at[y, pl.ds(0, 4), core, pl.ds(0, 2), pl.ds(0, 16)]
    return moved.at[pl.ds(0, 4), x, core, pl.ds(0, 2), pl.ds(16, 16)]


def send_messages(steps, gather, slots, outgoing, moved, sends, receives, own_sems):
    d = lax.axis_index("depth")
    for step in steps:
        for axis in range(2):
            for turn in range(2):
                index = 2 * step + turn
                target = line_tile(1 - axis, step, turn)
                fill_message(axis, index, target, gather, slots, outgoing)
                source = outgoing.at[axis, index]
                if index == 0:
                    pltpu.make_async_copy(source, message_target(axis, moved), own_sems.at[axis]).start()
                else:
                    remote(source, message_target(axis, moved), sends.at[axis], receives.at[axis], (d, target)).start()


def ring_copy(i, plan):
    source, target, _, send, receive, group = plan
    d, t, chip, core = place()
    if group == 8:
        me = d * 2 + core
        peer = (me + i) % 8
        device = (peer // 2, chip + peer % 2)
    else:
        me = t // 2
        peer = (me + i) % 16
        device = (d, 2 * peer + core)
    return remote(source(me, peer), target(me, peer), send, receive, device)


def start_all(plan):
    def step(i, carry):
        ring_copy(i, plan).start()
        return carry

    lax.fori_loop(1, plan[-1], step, 0)


def all_of(whole, send, receive):
    d, t, _, _ = place()
    return remote(whole, whole, send, receive, (d, (t + 1) % TILES))


def wait_arrived(plan):
    all_of(plan[2], plan[3], plan[4]).wait_recv()


def wait_sent(plan):
    all_of(plan[2], plan[3], plan[4]).wait_send()


def reduce_plans(packed, land_a, part, land_b, result, sems):
    a_send, a_receive, b_send, b_receive, c_send, c_receive = sems
    first = (
        lambda me, peer: packed.at[pl.ds(4 * peer, 4)], lambda me, peer: land_a.at[me], land_a.at[pl.ds(0, 7)],
        a_send, a_receive, 8,
    )
    second = (lambda me, peer: part, lambda me, peer: land_b.at[me], land_b.at[pl.ds(0, 15)], b_send, b_receive, 16)
    third = (
        lambda me, peer: land_b.at[16], lambda me, peer: result.at[pl.ds(4 * me, 4)], result.at[pl.ds(0, 28)],
        c_send, c_receive, 8,
    )
    return first, second, third


def reduce_first(plans, packed, land_a, part, land_b):
    d, t, chip, core = place()
    me = d * 2 + core
    wait_arrived(plans[0])
    land_a[me] = packed[pl.ds(4 * me, 4)]
    total = land_a[0]
    for j in range(1, 8):
        total += land_a[j]
    part[...] = total
    land_b[t // 2] = total
    start_all(plans[1])


def reduce_second(plans, part, land_b, result, factor):
    d, t, chip, core = place()
    me = d * 2 + core
    wait_arrived(plans[1])
    total = land_b[0]
    for j in range(1, 16):
        total += land_b[j]
    total = total * factor
    land_b[16] = total
    result[pl.ds(4 * me, 4)] = total
    start_all(plans[2])


def unpack_gradient(result, out, w):
    for r in range(27):
        tile = result[r]
        for g in range(4):
            t = 27 * g + r
            moved = tile if g == 0 else pltpu.roll(tile, 128 - 32 * g, 1)
            out[w, t // 4, pl.ds(8 * (t % 4), 8), :] = moved[:, :32]


def kernel(
    features_in, cotangent_in, first_in, second_in, links_in, depth_in, tile_in, workers_in,
    moved, gradients_out,
    features, cotangent, first_weight, second_weight, links, send_depth, send_tile, gradients,
    table_x, table_g, even_x, odd_x, even_g, odd_g, wide_first, wide_second, pre, back, hidden, folded,
    grad_pre, grad_input, gather, outgoing, names_land, names, slots,
    stage_d, land_d, stage_t, land_t, sections,
    stage_d2, land_d2, stage_t2, land_t2, sections2,
    packed, land_a, part, land_b, result,
    d_send, d_receive, t_send, t_receive, d2_send, d2_receive, t2_send, t2_receive,
    load_sem, store_sem, m_send, m_receive, own_sem, g_send, g_receive, n_send, n_receive, n_own, n_sem, a_send, a_receive, b_send, b_receive, c_send, c_receive, round_sem,
):
    d, t, chip, core = place()
    fields, tables = (features, cotangent), (table_x, table_g)
    pairs = (
        (features_in, features), (cotangent_in, cotangent), (depth_in, send_depth), (tile_in, send_tile),
        (links_in, links), (first_in, first_weight), (second_in, second_weight),
    )
    loads = [pltpu.make_async_copy(source, target, load_sem.at[i]) for i, (source, target) in enumerate(pairs)]
    for load in loads:
        load.start()
    barrier, greetings = greet()
    for load in loads:
        load.wait()
    stage_depth(fields, send_depth, stage_d)
    pl.semaphore_wait(barrier, greetings)
    along_depth = depth_copies(stage_d, land_d, d_send, d_receive)
    for copy in along_depth:
        copy.start()
    table_own(fields, tables)
    table_x[16] = jnp.zeros((64, 8, 128), F32)
    table_g[16] = jnp.zeros((64, 8, 128), F32)
    spread_weight(first_weight, wide_first)
    spread_word(round_sem, 0)
    for copy in along_depth:
        copy.wait()
    accept_depth(fields, land_d, sections, tables)
    stage_tile(2, sections, send_tile, stage_t)
    along_tile = tile_copies(stage_t, land_t, t_send, t_receive)
    for copy in along_tile:
        copy.start()
    table_depth(sections, tables)
    spread_weight(second_weight, wide_second)
    spread_word(round_sem, 1)
    for copy in along_tile:
        copy.wait()
    table_tile(land_t, tables)
    build_shifts(table_x, links, even_x, odd_x)
    spread_word(round_sem, 2)
    build_shifts(table_g, links, even_g, odd_g)
    spread_word(round_sem, 3)
    pre[...] = jnp.zeros((512, 256), F32)
    back[...] = jnp.zeros((512, 256), F32)
    conv_forward(even_x, odd_x, wide_first, pre)
    spread_word(round_sem, 4)
    conv_backward(even_g, odd_g, wide_second, back)
    spread_word(round_sem, 5)
    value = pre[...]
    sigma = 1.0 / (1.0 + jnp.exp(-value))
    hidden[...] = (value * sigma).T.astype(BF16)
    grad_pre[...] = (back[...] * sigma * (1.0 + value * (1.0 - sigma))).T.astype(BF16).reshape(8, 32, 512)

    stage_depth((grad_pre,), send_depth, stage_d2)
    along_depth = depth_copies(stage_d2, land_d2, d2_send, d2_receive)
    for copy in along_depth:
        copy.start()
    weight_gradient(lambda: hidden[...], even_g, odd_g, folded)
    spread_word(round_sem, 6)
    remotes, owns = share_workers(workers_in, names_land, n_send, n_receive, n_own)
    for copy in remotes + owns:
        copy.start()
    for copy in along_depth:
        copy.wait()
    accept_depth((grad_pre,), land_d2, sections2, tables)
    stage_tile(1, sections2, send_tile, stage_t2)
    along_tile = tile_copies(stage_t2, land_t2, t2_send, t2_receive)
    for copy in along_tile:
        copy.start()
    pack_gradient(folded, packed.at[1])
    plans = [
        reduce_plans(
            packed.at[w], land_a.at[w], part.at[w], land_b.at[w], result.at[w],
            tuple(s.at[w] for s in (a_send, a_receive, b_send, b_receive, c_send, c_receive)),
        )
        for w in range(2)
    ]
    start_all(plans[1][0])
    table_own((grad_pre,), tables[:1])
    table_depth(sections2, tables[:1])
    for copy in along_tile:
        copy.wait()
    table_tile(land_t2, tables[:1])
    build_shifts(table_x, links, even_x, odd_x)
    back[...] = jnp.zeros((512, 256), F32)
    conv_backward(even_x, odd_x, wide_first, back)
    reduce_first(plans[1], packed.at[1], land_a.at[1], part.at[1], land_b.at[1])
    grad_input[...] = (back[...].T.reshape(8, 32, 512) + cotangent[...].astype(F32)).astype(BF16)
    for step in (1, 3, 2):
        for axis in range(2):
            broadcast_copy(axis, step, grad_input, gather, g_send, g_receive).start()
    for axis in range(2):
        gather[axis, line_place(axis), 0:8] = grad_input[:, 16 * axis : 16 * axis + 16]
        for source in range(4):
            gather[axis, source, 8] = jnp.zeros((16, 512), BF16)
    all_names = all_of(names_land.at[pl.ds(0, 6)], n_send, n_receive)
    all_names.wait_recv()
    for copy in owns:
        copy.wait()
    to_scalar = pltpu.make_async_copy(names_land, names, n_sem)
    to_scalar.start()
    to_scalar.wait()
    find_slots(names, slots)

    factor = float(DEPTHS * TILES * 8 * 512) ** (-0.5)
    weight_gradient(lambda: features[...].reshape(256, 512), even_x, odd_x, folded)
    pack_gradient(folded, packed.at[0])
    start_all(plans[0][0])
    for axis in range(2):
        all_of(gather.at[axis, pl.ds(0, 3), pl.ds(0, 8)], g_send.at[axis], g_receive.at[axis]).wait_recv()
    parts = (gather, slots, outgoing, moved, m_send, m_receive, own_sem)
    send_messages((2,), *parts)
    reduce_second(plans[1], part.at[1], land_b.at[1], result.at[1], factor)
    reduce_first(plans[0], packed.at[0], land_a.at[0], part.at[0], land_b.at[0])
    send_messages((1, 3), *parts)
    wait_arrived(plans[1][2])
    unpack_gradient(result.at[1], gradients, 1)
    reduce_second(plans[0], part.at[0], land_b.at[0], result.at[0], factor)
    send_messages((0,), *parts)
    wait_arrived(plans[0][2])
    unpack_gradient(result.at[0], gradients, 0)
    store = pltpu.make_async_copy(gradients, gradients_out, store_sem)
    store.start()
    for w in range(2):
        for plan in plans[w]:
            wait_sent(plan)
    all_names.wait_send()
    for axis in range(2):
        all_of(gather.at[axis, pl.ds(0, 3), pl.ds(0, 8)], g_send.at[axis], g_receive.at[axis]).wait_send()
        pltpu.make_async_copy(outgoing.at[axis, 0], message_target(axis, moved), own_sem.at[axis]).wait()
        messages = all_of(outgoing.at[axis, pl.ds(1, 7)], m_send.at[axis], m_receive.at[axis])
        messages.wait_send()
        messages.wait_recv()
    store.wait()


def hand_over(moved_in, gradients_in, moved, gradients, held, held_gradients, in_sems, out_sems):
    spans = [(moved_in, held, moved, pl.ds(8 * i, 8)) for i in range(8)]
    spans += [(gradients_in, held_gradients, gradients, pl.ds(i, 1)) for i in range(2)]
    loads = [pltpu.make_async_copy(a.at[at], b.at[at], in_sems.at[i]) for i, (a, b, c, at) in enumerate(spans)]
    stores = [pltpu.make_async_copy(b.at[at], c.at[at], out_sems.at[i]) for i, (a, b, c, at) in enumerate(spans)]
    for load in loads:
        load.start()
    for load, store in zip(loads, stores):
        load.wait()
        store.start()
    for store in stores:
        store.wait()


def local(features, cotangent, first_weight, second_weight, neighbours, send_depth, send_tile, worker_tile):
    anywhere = pl.BlockSpec(memory_space=pl.ANY)
    brick = (32, 512)
    shifts = [pltpu.VMEM((3, 10, 80, 256), BF16), pltpu.VMEM((3, 10, 64, 256), BF16)]

    def halo(count):
        return [pltpu.VMEM((2, 2 * count, *brick), BF16)] * 4 + [pltpu.VMEM((count, 12, *brick), BF16)]

    dma = pltpu.SemaphoreType.DMA
    results = pl.pallas_call(
        kernel,
        out_shape=(
            jax.ShapeDtypeStruct((4, 4, 2, 2, *brick), BF16),
            jax.ShapeDtypeStruct((2, 27, 32, 32), F32),
        ),
        in_specs=[anywhere] * 8,
        out_specs=(anywhere, anywhere),
        scratch_shapes=[pltpu.VMEM((8, *brick), BF16)] * 2
        + [pltpu.VMEM((27, 32, 32), BF16)] * 2
        + [pltpu.SMEM((8, 26), jnp.int32), pltpu.SMEM((1, 2, 2), jnp.int32), pltpu.SMEM((1, 2, 2), jnp.int32)]
        + [pltpu.VMEM((2, 27, 32, 32), F32)]
        + [pltpu.VMEM((17, 64, 8, 128), F32)] * 2
        + shifts * 2
        + [pltpu.VMEM((3, 2304, 256), BF16)] * 2
        + [pltpu.VMEM((512, 256), F32)] * 2
        + [pltpu.VMEM((256, 512), BF16), pltpu.VMEM((864, 128), F32)]
        + [pltpu.VMEM((8, *brick), BF16), pltpu.VMEM((8, *brick), BF16)]
        + [pltpu.VMEM((2, 4, 9, 16, 512), BF16), pltpu.VMEM((2, 8, 4, 2, 16, 512), BF16)]
        + [pltpu.VMEM((8, 1, 8), jnp.int32), pltpu.SMEM((8, 1, 8), jnp.int32), pltpu.SMEM((8, 8), jnp.int32)]
        + halo(2)
        + halo(1)
        + [
            pltpu.VMEM((2, 32, 8, 128), F32),
            pltpu.VMEM((2, 8, 4, 8, 128), F32),
            pltpu.VMEM((2, 4, 8, 128), F32),
            pltpu.VMEM((2, 17, 4, 8, 128), F32),
            pltpu.VMEM((2, 32, 8, 128), F32),
        ]
        + [dma((2,))] * 8
        + [dma((7,)), dma]
        + [dma((2,))] * 5
        + [dma, dma, dma((2,)), dma]
        + [dma((2,))] * 6
        + [pltpu.SemaphoreType.REGULAR((6,))],
        compiler_params=pltpu.CompilerParams(
            collective_id=0, has_side_effects=True, vmem_limit_bytes=64 * 2**20 - 2**17
        ),
    )(features, cotangent, first_weight, second_weight, neighbours, send_depth, send_tile, worker_tile.reshape(1, 8))
    results = (results[0].reshape(2 * TILES, *brick), results[1])
    return pl.pallas_call(
        hand_over,
        out_shape=tuple(jax.ShapeDtypeStruct(r.shape, r.dtype) for r in results),
        in_specs=[anywhere] * 2,
        out_specs=(anywhere, anywhere),
        scratch_shapes=[pltpu.VMEM((2 * TILES, *brick), BF16), pltpu.VMEM((2, 27, 32, 32), F32), dma((10,)), dma((10,))],
        compiler_params=pltpu.CompilerParams(vmem_limit_bytes=64 * 2**20 - 2**17),
    )(*results)


def solution(mesh):
    rows = P(("depth", "tile"))
    placed = (rows, rows, P(), P(), rows, rows, rows, rows)
    return jax.shard_map(local, mesh=mesh, in_specs=placed, out_specs=(rows, P()), check_vma=False)
```

```python
import jax
import jax.numpy as jnp
from jax import lax
from jax.experimental import pallas as pl
from jax.experimental.pallas import tpu as pltpu
from jax.sharding import PartitionSpec as P

F32 = jnp.float32
BF16 = jnp.bfloat16


def iota(shape, dim):
    return lax.broadcasted_iota(jnp.int32, shape, dim)


def tiled_identity(lanes):
    return jnp.where(iota((32, lanes), 1) % 32 == iota((32, lanes), 0), 1.0, 0.0).astype(BF16)


def fill_table(table, slot, brick):
    spread = lax.dot_general(brick, tiled_identity(128), (((0,), (0,)), ((), ())), preferred_element_type=F32)
    table[slot] = spread.reshape(64, 8, 128)


def spread_weight(weight, wide):
    columns = iota((32, 256), 1) // 32
    rows = jnp.dot(weight[...].reshape(864, 32), tiled_identity(256), preferred_element_type=F32).astype(BF16)
    for k in range(27):
        for n in range(8):
            part = jnp.where(columns == n, rows[32 * k : 32 * k + 32], jnp.zeros((), BF16))
            wide[k // 9, pl.ds(256 * (k % 9) + 32 * n, 32), :] = part


def build_shifts(table, links, even, odd):
    lane = iota((8, 128), 1)
    sub = iota((8, 128), 0)

    def one_plane(a_block, a_source, a_row):
        entry = {}
        for rest in range(9):
            k = a_block * 9 + rest
            for n in range(8):
                if k == 13:
                    entry[rest, n] = n
                else:
                    link = links[n, k - (k > 13)]
                    entry[rest, n] = jnp.where(link < 0, 16, link)

        for half in range(2):
            def mixed(rest, b_source):
                parts = [table[entry[rest, 4 * half + j], a_source * 8 + b_source] for j in range(4)]
                low = jnp.where(lane < 32, parts[0], parts[1])
                high = jnp.where(lane < 96, parts[2], parts[3])
                return jnp.where(lane < 64, low, high)

            columns = pl.ds(128 * half, 128)
            rows = []
            for b in range(10):
                b_block, b_source = (b + 7) // 8, (b + 7) % 8
                mid = mixed(b_block * 3 + 1, b_source)
                lower = mixed(b_block * 3, b_source)
                upper = mixed(b_block * 3 + 2, b_source)
                down = pltpu.roll(jnp.where(sub == 7, lower, mid), 1, 0)
                up = pltpu.roll(jnp.where(sub == 0, upper, mid), 7, 0)
                rows.append((down, mid, up))
                if b > 0:
                    for v in range(3):
                        pair = jnp.concatenate([rows[b - 1][v], rows[b][v]], 0).astype(BF16)
                        if b % 2:
                            even[v, a_row, pl.ds(8 * (b - 1), 16), columns] = pair
                        else:
                            odd[v, a_row, pl.ds(8 * (b - 2), 16), columns] = pair

    one_plane(0, 7, 0)

    def middle(a, carry):
        one_plane(1, a, a + 1)
        return carry

    lax.fori_loop(0, 8, middle, 0)
    one_plane(2, 0, 9)


def piece(even, odd, a, rest):
    b, c = rest // 3, rest % 3
    source = odd[c, pl.ds(a, 8)] if b == 1 else even[c, pl.ds(a, 8), pl.ds(8 * b, 64)]
    return source.reshape(512, 256)


def conv_forward(even, odd, wide, total):
    def step(a, carry):
        left = jnp.concatenate([piece(even, odd, a, rest) for rest in range(9)], 1)
        total[...] += jnp.dot(left, wide[a], preferred_element_type=F32)
        return carry

    lax.fori_loop(0, 3, step, 0)


def conv_backward(even, odd, wide, total):
    def step(a, carry):
        acc = total[...]
        for rest in range(9):
            acc += lax.dot_general(
                piece(even, odd, a, rest), wide[2 - a, pl.ds(256 * (8 - rest), 256), :], (((1,), (1,)), ((), ())), preferred_element_type=F32
            )
        total[...] = acc
        return carry

    lax.fori_loop(0, 3, step, 0)


def weight_gradient(left_of, even, odd, folded):
    lane = iota((32, 128), 1)

    def step(a, carry):
        for rest in range(9):
            full = jnp.dot(left_of(), piece(even, odd, a, rest), preferred_element_type=F32)
            halves = []
            for half in range(2):
                parts = [full[128 * half + 32 * j : 128 * half + 32 * j + 32, 128 * half : 128 * half + 128] for j in range(4)]
                low = jnp.where(lane < 32, parts[0], parts[1])
                high = jnp.where(lane < 96, parts[2], parts[3])
                halves.append(jnp.where(lane < 64, low, high))
            both = halves[0] + halves[1]
            both = both + pltpu.roll(both, 64, 1)
            both = both + pltpu.roll(both, 32, 1)
            folded[pl.ds(pl.multiple_of(32 * (9 * (2 - a) + 8 - rest), 32), 32), :] = both
        return carry

    lax.fori_loop(0, 3, step, 0)


def pack_gradient(folded, packed):
    lane = iota((8, 128), 1)
    for r in range(27):
        parts = [folded[pl.ds(8 * (27 * g + r), 8), :] for g in range(4)]
        low = jnp.where(lane < 32, parts[0], parts[1])
        high = jnp.where(lane < 96, parts[2], parts[3])
        packed[r] = jnp.where(lane < 64, low, high)
    packed[27:32] = jnp.zeros((5, 8, 128), F32)

MESH = pl.DeviceIdType.MESH
DEPTHS, TILES = 4, 32


def remote(source, target, send, receive, device):
    return pltpu.make_async_remote_copy(
        src_ref=source, dst_ref=target, send_sem=send, recv_sem=receive, device_id=device, device_id_type=MESH
    )


def place():
    d, t = lax.axis_index("depth"), lax.axis_index("tile")
    return d, t, (t // 2) * 2, t % 2


def flipped(value, bit):
    step = 2**bit
    return value + step - 2 * step * ((value // step) % 2)


def greet():
    d, t, chip, core = place()
    barrier = pltpu.get_barrier_semaphore()
    peers = [(d, flipped(t, bit)) for bit in range(5)]
    peers += [(d, (t + 1) % TILES), (d, (t + TILES - 1) % TILES)]
    peers += [((d + step) % DEPTHS, t) for step in range(1, DEPTHS)]
    for peer in peers:
        pl.semaphore_signal(barrier, inc=1, device_id=peer, device_id_type=MESH)
    return barrier, len(peers)


def spread_word(round_sem, step):
    d, t, _, _ = place()
    if step > 0:
        pl.semaphore_wait(round_sem.at[step - 1], 1)
    if step < 6:
        peer = (d, flipped(t, step + 1)) if step < 4 else (flipped(d, step - 4), t)
        pl.semaphore_signal(round_sem.at[step], inc=1, device_id=peer, device_id_type=MESH)


def depth_copies(stage, land, sends, receives):
    d, t, _, _ = place()
    return (
        remote(stage.at[0], land.at[1], sends.at[0], receives.at[1], ((d + DEPTHS - 1) % DEPTHS, t)),
        remote(stage.at[1], land.at[0], sends.at[1], receives.at[0], ((d + 1) % DEPTHS, t)),
    )


def tile_copies(stage, land, sends, receives):
    d, t, _, _ = place()
    return (
        remote(stage.at[0], land.at[1], sends.at[0], receives.at[1], (d, (t + TILES - 1) % TILES)),
        remote(stage.at[1], land.at[0], sends.at[1], receives.at[0], (d, (t + 1) % TILES)),
    )


def stage_depth(fields, send_depth, stage):
    for side in range(2):
        for f, field in enumerate(fields):
            for j in range(2):
                stage[side, 2 * f + j] = field[send_depth[0, side, j]]


def accept_depth(fields, land, sections, tables):
    d, _, _, _ = place()
    inner = (d > 0, d < DEPTHS - 1)
    for f, field in enumerate(fields):
        sections[f, 0:8] = field[...]
        for side in range(2):
            for j in range(2):
                value = land[side, 2 * f + j]
                value = jnp.where(inner[side], value, jnp.zeros_like(value))
                sections[f, 8 + 2 * side + j] = value


def stage_tile(count, sections, send_tile, stage):
    for side in range(2):
        for f in range(count):
            for j in range(2):
                stage[side, 2 * f + j] = sections[f, send_tile[0, side, j]]


def table_own(fields, tables):
    for field, table in zip(fields, tables):
        for m in range(8):
            fill_table(table, m, field[m])


def table_depth(sections, tables):
    for f, table in enumerate(tables):
        for j in range(4):
            fill_table(table, 8 + j, sections[f, 8 + j])


def table_tile(land, tables):
    for f, table in enumerate(tables):
        for side in range(2):
            for j in range(2):
                fill_table(table, 12 + 2 * side + j, land[side, 2 * f + j])


def line_tile(axis, step, turn=0):
    t = lax.axis_index("tile")
    y, x, core = t // 8, (t // 2) % 4, (t + turn) % 2
    if axis == 0:
        return y * 8 + ((x + step) % 4) * 2 + core
    return ((y + step) % 4) * 8 + x * 2 + core


def line_place(axis):
    t = lax.axis_index("tile")
    return (t // 2) % 4 if axis == 0 else t // 8


def share_workers(workers_in, names_land, sends, receives, own_sems):
    d = lax.axis_index("depth")
    remotes, owns = [], []
    for axis in range(2):
        slot = names_land.at[4 * axis + line_place(axis)]
        owns.append(pltpu.make_async_copy(workers_in, slot, own_sems.at[axis]))
        for step in (1, 2, 3):
            remotes.append(remote(workers_in, slot, sends, receives, (d, line_tile(axis, step))))
    return remotes, owns


def broadcast_copy(axis, step, grad_input, gather, sends, receives):
    d = lax.axis_index("depth")
    return remote(
        grad_input.at[pl.ds(0, 8), pl.ds(16 * axis, 16)],
        gather.at[axis, line_place(axis), pl.ds(0, 8)],
        sends.at[axis],
        receives.at[axis],
        (d, line_tile(axis, step)),
    )


def find_slots(names, slots):
    for line in range(8):
        own = [names[line, 0, n] for n in range(8)]
        for n in range(8):
            rank = jnp.int32(0)
            for m in range(n):
                rank = rank + jnp.where(own[m] == own[n], 1, 0)
            slots[line, n] = 2 * own[n] + rank


def fill_message(axis, index, target, gather, slots, outgoing):
    for source in range(4):
        held = [slots[4 * axis + source, n] for n in range(8)]
        for q in range(2):
            key = 2 * target + q
            brick = jnp.int32(8)
            for n in range(8):
                brick = jnp.where(held[n] == key, n, brick)
            outgoing[axis, index, source, q] = gather[axis, source, brick]


def message_target(axis, moved):
    t = lax.axis_index("tile")
    y, x, core = t // 8, (t // 2) % 4, t % 2
    if axis == 0:
        return moved.at[y, pl.ds(0, 4), core, pl.ds(0, 2), pl.ds(0, 16)]
    return moved.at[pl.ds(0, 4), x, core, pl.ds(0, 2), pl.ds(16, 16)]


def send_messages(steps, gather, slots, outgoing, moved, sends, receives, own_sems):
    d = lax.axis_index("depth")
    for step in steps:
        for axis in range(2):
            for turn in range(2):
                index = 2 * step + turn
                target = line_tile(1 - axis, step, turn)
                fill_message(axis, index, target, gather, slots, outgoing)
                source = outgoing.at[axis, index]
                if index == 0:
                    pltpu.make_async_copy(source, message_target(axis, moved), own_sems.at[axis]).start()
                else:
                    remote(source, message_target(axis, moved), sends.at[axis], receives.at[axis], (d, target)).start()


def ring_copy(i, plan):
    source, target, _, send, receive, group = plan
    d, t, chip, core = place()
    if group == 8:
        me = d * 2 + core
        peer = (me + i) % 8
        device = (peer // 2, chip + peer % 2)
    else:
        me = t // 2
        peer = (me + i) % 16
        device = (d, 2 * peer + core)
    return remote(source(me, peer), target(me, peer), send, receive, device)


def start_all(plan):
    def step(i, carry):
        ring_copy(i, plan).start()
        return carry

    lax.fori_loop(1, plan[-1], step, 0)


def all_of(whole, send, receive):
    d, t, _, _ = place()
    return remote(whole, whole, send, receive, (d, (t + 1) % TILES))


def wait_arrived(plan):
    all_of(plan[2], plan[3], plan[4]).wait_recv()


def wait_sent(plan):
    all_of(plan[2], plan[3], plan[4]).wait_send()


def reduce_plans(packed, land_a, part, land_b, result, sems):
    a_send, a_receive, b_send, b_receive, c_send, c_receive = sems
    first = (
        lambda me, peer: packed.at[pl.ds(4 * peer, 4)], lambda me, peer: land_a.at[me], land_a.at[pl.ds(0, 7)],
        a_send, a_receive, 8,
    )
    second = (lambda me, peer: part, lambda me, peer: land_b.at[me], land_b.at[pl.ds(0, 15)], b_send, b_receive, 16)
    third = (
        lambda me, peer: land_b.at[16], lambda me, peer: result.at[pl.ds(4 * me, 4)], result.at[pl.ds(0, 28)],
        c_send, c_receive, 8,
    )
    return first, second, third


def reduce_first(plans, packed, land_a, part, land_b):
    d, t, chip, core = place()
    me = d * 2 + core
    wait_arrived(plans[0])
    land_a[me] = packed[pl.ds(4 * me, 4)]
    total = land_a[0]
    for j in range(1, 8):
        total += land_a[j]
    part[...] = total
    land_b[t // 2] = total
    start_all(plans[1])


def reduce_second(plans, part, land_b, result, factor):
    d, t, chip, core = place()
    me = d * 2 + core
    wait_arrived(plans[1])
    total = land_b[0]
    for j in range(1, 16):
        total += land_b[j]
    total = total * factor
    land_b[16] = total
    result[pl.ds(4 * me, 4)] = total
    start_all(plans[2])


def unpack_gradient(result, out, w):
    for r in range(27):
        tile = result[r]
        for g in range(4):
            t = 27 * g + r
            moved = tile if g == 0 else pltpu.roll(tile, 128 - 32 * g, 1)
            out[w, t // 4, pl.ds(8 * (t % 4), 8), :] = moved[:, :32]


def kernel(
    features_in, cotangent_in, first_in, second_in, links_in, depth_in, tile_in, workers_in,
    moved, gradients_out,
    features, cotangent, first_weight, second_weight, links, send_depth, send_tile, gradients,
    table_x, table_g, even_x, odd_x, even_g, odd_g, wide_first, wide_second, pre, back, hidden, folded,
    grad_pre, grad_input, gather, outgoing, names_land, names, slots,
    stage_d, land_d, stage_t, land_t, sections,
    stage_d1, land_d1, stage_t1, land_t1, sections1,
    stage_d2, land_d2, stage_t2, land_t2, sections2,
    packed, land_a, part, land_b, result,
    d_send, d_receive, t_send, t_receive, d1_send, d1_receive, t1_send, t1_receive, d2_send, d2_receive, t2_send, t2_receive,
    load_sem, store_sem, m_send, m_receive, own_sem, g_send, g_receive, n_send, n_receive, n_own, n_sem, a_send, a_receive, b_send, b_receive, c_send, c_receive, round_sem,
):
    d, t, chip, core = place()
    fields, tables = (features, cotangent), (table_x, table_g)
    pairs = (
        (features_in, features), (cotangent_in, cotangent), (depth_in, send_depth), (tile_in, send_tile),
        (links_in, links), (first_in, first_weight), (second_in, second_weight),
    )
    loads = [pltpu.make_async_copy(source, target, load_sem.at[i]) for i, (source, target) in enumerate(pairs)]
    for load in loads:
        load.start()
    barrier, greetings = greet()
    for load in loads:
        load.wait()
    stage_depth((features,), send_depth, stage_d)
    stage_depth((cotangent,), send_depth, stage_d1)
    pl.semaphore_wait(barrier, greetings)
    depth_x = depth_copies(stage_d, land_d, d_send, d_receive)
    depth_g = depth_copies(stage_d1, land_d1, d1_send, d1_receive)
    for copy in depth_x + depth_g:
        copy.start()
    table_own(fields, tables)
    table_x[16] = jnp.zeros((64, 8, 128), F32)
    table_g[16] = jnp.zeros((64, 8, 128), F32)
    spread_word(round_sem, 0)
    for copy in depth_x:
        copy.wait()
    accept_depth((features,), land_d, sections, tables)
    stage_tile(1, sections, send_tile, stage_t)
    tile_x = tile_copies(stage_t, land_t, t_send, t_receive)
    for copy in tile_x:
        copy.start()
    table_depth(sections, tables[:1])
    spread_weight(first_weight, wide_first)
    for copy in depth_g:
        copy.wait()
    accept_depth((cotangent,), land_d1, sections1, tables)
    stage_tile(1, sections1, send_tile, stage_t1)
    tile_g = tile_copies(stage_t1, land_t1, t1_send, t1_receive)
    for copy in tile_g:
        copy.start()
    spread_word(round_sem, 1)
    table_depth(sections1, tables[1:])
    for copy in tile_x:
        copy.wait()
    table_tile(land_t, tables[:1])
    build_shifts(table_x, links, even_x, odd_x)
    spread_word(round_sem, 2)
    pre[...] = jnp.zeros((512, 256), F32)
    back[...] = jnp.zeros((512, 256), F32)
    conv_forward(even_x, odd_x, wide_first, pre)
    spread_word(round_sem, 3)
    spread_weight(second_weight, wide_second)
    value = pre[...]
    sigma = 1.0 / (1.0 + jnp.exp(-value))
    hidden[...] = (value * sigma).T.astype(BF16)
    pre[...] = sigma * (1.0 + value * (1.0 - sigma))
    for copy in tile_g:
        copy.wait()
    table_tile(land_t1, tables[1:])
    build_shifts(table_g, links, even_g, odd_g)
    spread_word(round_sem, 4)
    conv_backward(even_g, odd_g, wide_second, back)
    spread_word(round_sem, 5)
    grad_pre[...] = (back[...] * pre[...]).T.astype(BF16).reshape(8, 32, 512)

    stage_depth((grad_pre,), send_depth, stage_d2)
    along_depth = depth_copies(stage_d2, land_d2, d2_send, d2_receive)
    for copy in along_depth:
        copy.start()
    weight_gradient(lambda: hidden[...], even_g, odd_g, folded)
    spread_word(round_sem, 6)
    remotes, owns = share_workers(workers_in, names_land, n_send, n_receive, n_own)
    for copy in remotes + owns:
        copy.start()
    for copy in along_depth:
        copy.wait()
    accept_depth((grad_pre,), land_d2, sections2, tables)
    stage_tile(1, sections2, send_tile, stage_t2)
    along_tile = tile_copies(stage_t2, land_t2, t2_send, t2_receive)
    for copy in along_tile:
        copy.start()
    pack_gradient(folded, packed.at[1])
    plans = [
        reduce_plans(
            packed.at[w], land_a.at[w], part.at[w], land_b.at[w], result.at[w],
            tuple(s.at[w] for s in (a_send, a_receive, b_send, b_receive, c_send, c_receive)),
        )
        for w in range(2)
    ]
    start_all(plans[1][0])
    table_own((grad_pre,), tables[:1])
    table_depth(sections2, tables[:1])
    for copy in along_tile:
        copy.wait()
    table_tile(land_t2, tables[:1])
    build_shifts(table_x, links, even_x, odd_x)
    back[...] = jnp.zeros((512, 256), F32)
    conv_backward(even_x, odd_x, wide_first, back)
    grad_input[...] = (back[...].T.reshape(8, 32, 512) + cotangent[...].astype(F32)).astype(BF16)
    for step in (1, 3, 2):
        for axis in range(2):
            broadcast_copy(axis, step, grad_input, gather, g_send, g_receive).start()
    for axis in range(2):
        gather[axis, line_place(axis), 0:8] = grad_input[:, 16 * axis : 16 * axis + 16]
        for source in range(4):
            gather[axis, source, 8] = jnp.zeros((16, 512), BF16)
    all_names = all_of(names_land.at[pl.ds(0, 6)], n_send, n_receive)
    all_names.wait_recv()
    for copy in owns:
        copy.wait()
    to_scalar = pltpu.make_async_copy(names_land, names, n_sem)
    to_scalar.start()
    to_scalar.wait()
    find_slots(names, slots)

    factor = float(DEPTHS * TILES * 8 * 512) ** (-0.5)
    reduce_first(plans[1], packed.at[1], land_a.at[1], part.at[1], land_b.at[1])
    weight_gradient(lambda: features[...].reshape(256, 512), even_x, odd_x, folded)
    pack_gradient(folded, packed.at[0])
    start_all(plans[0][0])
    for axis in range(2):
        all_of(gather.at[axis, pl.ds(0, 3), pl.ds(0, 8)], g_send.at[axis], g_receive.at[axis]).wait_recv()
    parts = (gather, slots, outgoing, moved, m_send, m_receive, own_sem)
    send_messages((2,), *parts)
    reduce_second(plans[1], part.at[1], land_b.at[1], result.at[1], factor)
    reduce_first(plans[0], packed.at[0], land_a.at[0], part.at[0], land_b.at[0])
    send_messages((1, 3), *parts)
    wait_arrived(plans[1][2])
    unpack_gradient(result.at[1], gradients, 1)
    reduce_second(plans[0], part.at[0], land_b.at[0], result.at[0], factor)
    send_messages((0,), *parts)
    wait_arrived(plans[0][2])
    unpack_gradient(result.at[0], gradients, 0)
    store = pltpu.make_async_copy(gradients, gradients_out, store_sem)
    store.start()
    for w in range(2):
        for plan in plans[w]:
            wait_sent(plan)
    all_names.wait_send()
    for axis in range(2):
        all_of(gather.at[axis, pl.ds(0, 3), pl.ds(0, 8)], g_send.at[axis], g_receive.at[axis]).wait_send()
        pltpu.make_async_copy(outgoing.at[axis, 0], message_target(axis, moved), own_sem.at[axis]).wait()
        messages = all_of(outgoing.at[axis, pl.ds(1, 7)], m_send.at[axis], m_receive.at[axis])
        messages.wait_send()
        messages.wait_recv()
    store.wait()


def hand_over(moved_in, gradients_in, moved, gradients, held, held_gradients, in_sems, out_sems):
    spans = [(moved_in, held, moved, pl.ds(8 * i, 8)) for i in range(8)]
    spans += [(gradients_in, held_gradients, gradients, pl.ds(i, 1)) for i in range(2)]
    loads = [pltpu.make_async_copy(a.at[at], b.at[at], in_sems.at[i]) for i, (a, b, c, at) in enumerate(spans)]
    stores = [pltpu.make_async_copy(b.at[at], c.at[at], out_sems.at[i]) for i, (a, b, c, at) in enumerate(spans)]
    for load in loads:
        load.start()
    for load, store in zip(loads, stores):
        load.wait()
        store.start()
    for store in stores:
        store.wait()


def local(features, cotangent, first_weight, second_weight, neighbours, send_depth, send_tile, worker_tile):
    anywhere = pl.BlockSpec(memory_space=pl.ANY)
    brick = (32, 512)
    shifts = [pltpu.VMEM((3, 10, 80, 256), BF16), pltpu.VMEM((3, 10, 64, 256), BF16)]

    def halo(count):
        return [pltpu.VMEM((2, 2 * count, *brick), BF16)] * 4 + [pltpu.VMEM((count, 12, *brick), BF16)]

    dma = pltpu.SemaphoreType.DMA
    results = pl.pallas_call(
        kernel,
        out_shape=(
            jax.ShapeDtypeStruct((4, 4, 2, 2, *brick), BF16),
            jax.ShapeDtypeStruct((2, 27, 32, 32), F32),
        ),
        in_specs=[anywhere] * 8,
        out_specs=(anywhere, anywhere),
        scratch_shapes=[pltpu.VMEM((8, *brick), BF16)] * 2
        + [pltpu.VMEM((27, 32, 32), BF16)] * 2
        + [pltpu.SMEM((8, 26), jnp.int32), pltpu.SMEM((1, 2, 2), jnp.int32), pltpu.SMEM((1, 2, 2), jnp.int32)]
        + [pltpu.VMEM((2, 27, 32, 32), F32)]
        + [pltpu.VMEM((17, 64, 8, 128), F32)] * 2
        + shifts * 2
        + [pltpu.VMEM((3, 2304, 256), BF16)] * 2
        + [pltpu.VMEM((512, 256), F32)] * 2
        + [pltpu.VMEM((256, 512), BF16), pltpu.VMEM((864, 128), F32)]
        + [pltpu.VMEM((8, *brick), BF16), pltpu.VMEM((8, *brick), BF16)]
        + [pltpu.VMEM((2, 4, 9, 16, 512), BF16), pltpu.VMEM((2, 8, 4, 2, 16, 512), BF16)]
        + [pltpu.VMEM((8, 1, 8), jnp.int32), pltpu.SMEM((8, 1, 8), jnp.int32), pltpu.SMEM((8, 8), jnp.int32)]
        + halo(1)
        + halo(1)
        + halo(1)
        + [
            pltpu.VMEM((2, 32, 8, 128), F32),
            pltpu.VMEM((2, 8, 4, 8, 128), F32),
            pltpu.VMEM((2, 4, 8, 128), F32),
            pltpu.VMEM((2, 17, 4, 8, 128), F32),
            pltpu.VMEM((2, 32, 8, 128), F32),
        ]
        + [dma((2,))] * 12
        + [dma((7,)), dma]
        + [dma((2,))] * 5
        + [dma, dma, dma((2,)), dma]
        + [dma((2,))] * 6
        + [pltpu.SemaphoreType.REGULAR((6,))],
        compiler_params=pltpu.CompilerParams(
            collective_id=0, has_side_effects=True, vmem_limit_bytes=64 * 2**20 - 2**17
        ),
    )(features, cotangent, first_weight, second_weight, neighbours, send_depth, send_tile, worker_tile.reshape(1, 8))
    results = (results[0].reshape(2 * TILES, *brick), results[1])
    return pl.pallas_call(
        hand_over,
        out_shape=tuple(jax.ShapeDtypeStruct(r.shape, r.dtype) for r in results),
        in_specs=[anywhere] * 2,
        out_specs=(anywhere, anywhere),
        scratch_shapes=[pltpu.VMEM((2 * TILES, *brick), BF16), pltpu.VMEM((2, 27, 32, 32), F32), dma((10,)), dma((10,))],
        compiler_params=pltpu.CompilerParams(vmem_limit_bytes=64 * 2**20 - 2**17),
    )(*results)


def solution(mesh):
    rows = P(("depth", "tile"))
    placed = (rows, rows, P(), P(), rows, rows, rows, rows)
    return jax.shard_map(local, mesh=mesh, in_specs=placed, out_specs=(rows, P()), check_vma=False)
```

```python
import jax
import jax.numpy as jnp
from jax import lax
from jax.experimental import pallas as pl
from jax.experimental.pallas import tpu as pltpu
from jax.sharding import PartitionSpec as P

F32 = jnp.float32
BF16 = jnp.bfloat16


def iota(shape, dim):
    return lax.broadcasted_iota(jnp.int32, shape, dim)


def tiled_identity(lanes):
    return jnp.where(iota((32, lanes), 1) % 32 == iota((32, lanes), 0), 1.0, 0.0).astype(BF16)


def fill_table(table, slot, brick):
    spread = lax.dot_general(brick, tiled_identity(128), (((0,), (0,)), ((), ())), preferred_element_type=F32)
    table[slot] = spread.reshape(64, 8, 128)


def spread_weight(weight, wide):
    columns = iota((32, 256), 1) // 32
    rows = jnp.dot(weight[...].reshape(864, 32), tiled_identity(256), preferred_element_type=F32).astype(BF16)
    for k in range(27):
        for n in range(8):
            part = jnp.where(columns == n, rows[32 * k : 32 * k + 32], jnp.zeros((), BF16))
            wide[k // 9, pl.ds(256 * (k % 9) + 32 * n, 32), :] = part


def build_shifts(table, links, even, odd):
    lane = iota((8, 128), 1)
    sub = iota((8, 128), 0)

    def one_plane(a_block, a_source, a_row):
        entry = {}
        for rest in range(9):
            k = a_block * 9 + rest
            for n in range(8):
                if k == 13:
                    entry[rest, n] = n
                else:
                    link = links[n, k - (k > 13)]
                    entry[rest, n] = jnp.where(link < 0, 16, link)

        for half in range(2):
            def mixed(rest, b_source):
                parts = [table[entry[rest, 4 * half + j], a_source * 8 + b_source] for j in range(4)]
                low = jnp.where(lane < 32, parts[0], parts[1])
                high = jnp.where(lane < 96, parts[2], parts[3])
                return jnp.where(lane < 64, low, high)

            columns = pl.ds(128 * half, 128)
            rows = []
            for b in range(10):
                b_block, b_source = (b + 7) // 8, (b + 7) % 8
                mid = mixed(b_block * 3 + 1, b_source)
                lower = mixed(b_block * 3, b_source)
                upper = mixed(b_block * 3 + 2, b_source)
                down = pltpu.roll(jnp.where(sub == 7, lower, mid), 1, 0)
                up = pltpu.roll(jnp.where(sub == 0, upper, mid), 7, 0)
                rows.append((down, mid, up))
                if b > 0:
                    for v in range(3):
                        pair = jnp.concatenate([rows[b - 1][v], rows[b][v]], 0).astype(BF16)
                        if b % 2:
                            even[v, a_row, pl.ds(8 * (b - 1), 16), columns] = pair
                        else:
                            odd[v, a_row, pl.ds(8 * (b - 2), 16), columns] = pair

    one_plane(0, 7, 0)

    def middle(a, carry):
        one_plane(1, a, a + 1)
        return carry

    lax.fori_loop(0, 8, middle, 0)
    one_plane(2, 0, 9)


def piece(even, odd, a, rest):
    b, c = rest // 3, rest % 3
    source = odd[c, pl.ds(a, 8)] if b == 1 else even[c, pl.ds(a, 8), pl.ds(8 * b, 64)]
    return source.reshape(512, 256)


def conv_forward(even, odd, wide, total):
    def step(a, carry):
        left = jnp.concatenate([piece(even, odd, a, rest) for rest in range(9)], 1)
        total[...] += jnp.dot(left, wide[a], preferred_element_type=F32)
        return carry

    lax.fori_loop(0, 3, step, 0)


def conv_backward(even, odd, wide, total):
    def step(a, carry):
        acc = total[...]
        for rest in range(9):
            acc += lax.dot_general(
                piece(even, odd, a, rest), wide[2 - a, pl.ds(256 * (8 - rest), 256), :], (((1,), (1,)), ((), ())), preferred_element_type=F32
            )
        total[...] = acc
        return carry

    lax.fori_loop(0, 3, step, 0)


def weight_gradient(left_of, even, odd, folded):
    lane = iota((32, 128), 1)

    def step(a, carry):
        for rest in range(9):
            full = jnp.dot(left_of(), piece(even, odd, a, rest), preferred_element_type=F32)
            halves = []
            for half in range(2):
                parts = [full[128 * half + 32 * j : 128 * half + 32 * j + 32, 128 * half : 128 * half + 128] for j in range(4)]
                low = jnp.where(lane < 32, parts[0], parts[1])
                high = jnp.where(lane < 96, parts[2], parts[3])
                halves.append(jnp.where(lane < 64, low, high))
            both = halves[0] + halves[1]
            both = both + pltpu.roll(both, 64, 1)
            both = both + pltpu.roll(both, 32, 1)
            folded[pl.ds(pl.multiple_of(32 * (9 * (2 - a) + 8 - rest), 32), 32), :] = both
        return carry

    lax.fori_loop(0, 3, step, 0)


def pack_gradient(folded, packed):
    lane = iota((8, 128), 1)
    for r in range(27):
        parts = [folded[pl.ds(8 * (27 * g + r), 8), :] for g in range(4)]
        low = jnp.where(lane < 32, parts[0], parts[1])
        high = jnp.where(lane < 96, parts[2], parts[3])
        packed[r] = jnp.where(lane < 64, low, high)
    packed[27:32] = jnp.zeros((5, 8, 128), F32)

MESH = pl.DeviceIdType.MESH
DEPTHS, TILES = 4, 32


def remote(source, target, send, receive, device):
    return pltpu.make_async_remote_copy(
        src_ref=source, dst_ref=target, send_sem=send, recv_sem=receive, device_id=device, device_id_type=MESH
    )


def place():
    d, t = lax.axis_index("depth"), lax.axis_index("tile")
    return d, t, (t // 2) * 2, t % 2


def flipped(value, bit):
    step = 2**bit
    return value + step - 2 * step * ((value // step) % 2)


def greet():
    d, t, chip, core = place()
    barrier = pltpu.get_barrier_semaphore()
    peers = [(d, flipped(t, bit)) for bit in range(5)]
    peers += [(d, (t + 1) % TILES), (d, (t + TILES - 1) % TILES)]
    peers += [((d + step) % DEPTHS, t) for step in range(1, DEPTHS)]
    for peer in peers:
        pl.semaphore_signal(barrier, inc=1, device_id=peer, device_id_type=MESH)
    return barrier, len(peers)


def spread_word(round_sem, step):
    d, t, _, _ = place()
    if step > 0:
        pl.semaphore_wait(round_sem.at[step - 1], 1)
    if step < 6:
        peer = (d, flipped(t, step + 1)) if step < 4 else (flipped(d, step - 4), t)
        pl.semaphore_signal(round_sem.at[step], inc=1, device_id=peer, device_id_type=MESH)


def depth_copies(stage, land, sends, receives):
    d, t, _, _ = place()
    return (
        remote(stage.at[0], land.at[1], sends.at[0], receives.at[1], ((d + DEPTHS - 1) % DEPTHS, t)),
        remote(stage.at[1], land.at[0], sends.at[1], receives.at[0], ((d + 1) % DEPTHS, t)),
    )


def tile_copies(stage, land, sends, receives):
    d, t, _, _ = place()
    return (
        remote(stage.at[0], land.at[1], sends.at[0], receives.at[1], (d, (t + TILES - 1) % TILES)),
        remote(stage.at[1], land.at[0], sends.at[1], receives.at[0], (d, (t + 1) % TILES)),
    )


def stage_depth(fields, send_depth, stage):
    for side in range(2):
        for f, field in enumerate(fields):
            for j in range(2):
                stage[side, 2 * f + j] = field[send_depth[0, side, j]]


def accept_depth(fields, land, sections, tables):
    d, _, _, _ = place()
    inner = (d > 0, d < DEPTHS - 1)
    for f, field in enumerate(fields):
        sections[f, 0:8] = field[...]
        for side in range(2):
            for j in range(2):
                value = land[side, 2 * f + j]
                value = jnp.where(inner[side], value, jnp.zeros_like(value))
                sections[f, 8 + 2 * side + j] = value


def stage_tile(count, sections, send_tile, stage):
    for side in range(2):
        for f in range(count):
            for j in range(2):
                stage[side, 2 * f + j] = sections[f, send_tile[0, side, j]]


def table_own(fields, tables):
    for field, table in zip(fields, tables):
        for m in range(8):
            fill_table(table, m, field[m])


def table_depth(sections, tables):
    for f, table in enumerate(tables):
        for j in range(4):
            fill_table(table, 8 + j, sections[f, 8 + j])


def table_tile(land, tables):
    for f, table in enumerate(tables):
        for side in range(2):
            for j in range(2):
                fill_table(table, 12 + 2 * side + j, land[side, 2 * f + j])


def line_tile(axis, step, turn=0):
    t = lax.axis_index("tile")
    y, x, core = t // 8, (t // 2) % 4, (t + turn) % 2
    if axis == 0:
        return y * 8 + ((x + step) % 4) * 2 + core
    return ((y + step) % 4) * 8 + x * 2 + core


def line_place(axis):
    t = lax.axis_index("tile")
    return (t // 2) % 4 if axis == 0 else t // 8


def share_workers(workers_in, names_land, sends, receives, own_sems):
    d = lax.axis_index("depth")
    remotes, owns = [], []
    for axis in range(2):
        slot = names_land.at[4 * axis + line_place(axis)]
        owns.append(pltpu.make_async_copy(workers_in, slot, own_sems.at[axis]))
        for step in (1, 2, 3):
            remotes.append(remote(workers_in, slot, sends, receives, (d, line_tile(axis, step))))
    return remotes, owns


def broadcast_copy(axis, step, grad_input, gather, sends, receives):
    d = lax.axis_index("depth")
    return remote(
        grad_input.at[pl.ds(0, 8), pl.ds(16 * axis, 16)],
        gather.at[axis, line_place(axis), pl.ds(0, 8)],
        sends.at[axis],
        receives.at[axis],
        (d, line_tile(axis, step)),
    )


def find_slots(names, slots):
    for line in range(8):
        own = [names[line, 0, n] for n in range(8)]
        for n in range(8):
            rank = jnp.int32(0)
            for m in range(n):
                rank = rank + jnp.where(own[m] == own[n], 1, 0)
            slots[line, n] = 2 * own[n] + rank


def fill_message(axis, index, target, gather, slots, outgoing):
    for source in range(4):
        held = [slots[4 * axis + source, n] for n in range(8)]
        for q in range(2):
            key = 2 * target + q
            brick = jnp.int32(8)
            for n in range(8):
                brick = jnp.where(held[n] == key, n, brick)
            outgoing[axis, index, source, q] = gather[axis, source, brick]


def message_target(axis, moved):
    t = lax.axis_index("tile")
    y, x, core = t // 8, (t // 2) % 4, t % 2
    if axis == 0:
        return moved.at[y, pl.ds(0, 4), core, pl.ds(0, 2), pl.ds(0, 16)]
    return moved.at[pl.ds(0, 4), x, core, pl.ds(0, 2), pl.ds(16, 16)]


def send_messages(steps, gather, slots, outgoing, moved, sends, receives, own_sems):
    d = lax.axis_index("depth")
    for step in steps:
        for axis in range(2):
            for turn in range(2):
                index = 2 * step + turn
                target = line_tile(1 - axis, step, turn)
                fill_message(axis, index, target, gather, slots, outgoing)
                source = outgoing.at[axis, index]
                if index == 0:
                    pltpu.make_async_copy(source, message_target(axis, moved), own_sems.at[axis]).start()
                else:
                    remote(source, message_target(axis, moved), sends.at[axis], receives.at[axis], (d, target)).start()


def ring_copy(i, plan):
    source, target, _, send, receive, group = plan
    d, t, chip, core = place()
    if group == 8:
        me = d * 2 + core
        peer = (me + i) % 8
        device = (peer // 2, chip + peer % 2)
    else:
        me = t // 2
        peer = (me + i) % 16
        device = (d, 2 * peer + core)
    return remote(source(me, peer), target(me, peer), send, receive, device)


def start_all(plan):
    def step(i, carry):
        ring_copy(i, plan).start()
        return carry

    lax.fori_loop(1, plan[-1], step, 0)


def all_of(whole, send, receive):
    d, t, _, _ = place()
    return remote(whole, whole, send, receive, (d, (t + 1) % TILES))


def wait_arrived(plan):
    all_of(plan[2], plan[3], plan[4]).wait_recv()


def wait_sent(plan):
    all_of(plan[2], plan[3], plan[4]).wait_send()


def reduce_plans(packed, land_a, part, land_b, result, sems):
    a_send, a_receive, b_send, b_receive, c_send, c_receive = sems
    first = (
        lambda me, peer: packed.at[pl.ds(4 * peer, 4)], lambda me, peer: land_a.at[me], land_a.at[pl.ds(0, 7)],
        a_send, a_receive, 8,
    )
    second = (lambda me, peer: part, lambda me, peer: land_b.at[me], land_b.at[pl.ds(0, 15)], b_send, b_receive, 16)
    third = (
        lambda me, peer: land_b.at[16], lambda me, peer: result.at[pl.ds(4 * me, 4)], result.at[pl.ds(0, 28)],
        c_send, c_receive, 8,
    )
    return first, second, third


def reduce_first(plans, packed, land_a, part, land_b):
    d, t, chip, core = place()
    me = d * 2 + core
    wait_arrived(plans[0])
    land_a[me] = packed[pl.ds(4 * me, 4)]
    total = land_a[0]
    for j in range(1, 8):
        total += land_a[j]
    part[...] = total
    land_b[t // 2] = total
    start_all(plans[1])


def reduce_second(plans, part, land_b, result, factor):
    d, t, chip, core = place()
    me = d * 2 + core
    wait_arrived(plans[1])
    total = land_b[0]
    for j in range(1, 16):
        total += land_b[j]
    total = total * factor
    land_b[16] = total
    result[pl.ds(4 * me, 4)] = total
    start_all(plans[2])


def unpack_gradient(result, out, w):
    for r in range(27):
        tile = result[r]
        for g in range(4):
            t = 27 * g + r
            moved = tile if g == 0 else pltpu.roll(tile, 128 - 32 * g, 1)
            out[w, t // 4, pl.ds(8 * (t % 4), 8), :] = moved[:, :32]


def kernel(
    features_in, cotangent_in, first_in, second_in, links_in, depth_in, tile_in, workers_in,
    moved, gradients_out,
    features, cotangent, first_weight, second_weight, links, send_depth, send_tile, gradients,
    table_x, table_g, even_x, odd_x, even_g, odd_g, wide_first, wide_second, pre, back, hidden, folded,
    grad_pre, grad_input, gather, outgoing, names_land, names, slots,
    stage_d, land_d, stage_t, land_t, sections,
    stage_d1, land_d1, stage_t1, land_t1, sections1,
    stage_d2, land_d2, stage_t2, land_t2, sections2,
    packed, land_a, part, land_b, result,
    d_send, d_receive, t_send, t_receive, d1_send, d1_receive, t1_send, t1_receive, d2_send, d2_receive, t2_send, t2_receive,
    load_sem, store_sem, m_send, m_receive, own_sem, g_send, g_receive, n_send, n_receive, n_own, n_sem, a_send, a_receive, b_send, b_receive, c_send, c_receive, round_sem,
):
    d, t, chip, core = place()
    fields, tables = (features, cotangent), (table_x, table_g)
    pairs = (
        (features_in, features), (cotangent_in, cotangent), (depth_in, send_depth), (tile_in, send_tile),
        (links_in, links), (first_in, first_weight), (second_in, second_weight),
    )
    loads = [pltpu.make_async_copy(source, target, load_sem.at[i]) for i, (source, target) in enumerate(pairs)]
    for load in loads:
        load.start()
    barrier, greetings = greet()
    for load in loads:
        load.wait()
    stage_depth((features,), send_depth, stage_d)
    stage_depth((cotangent,), send_depth, stage_d1)
    pl.semaphore_wait(barrier, greetings)
    depth_x = depth_copies(stage_d, land_d, d_send, d_receive)
    depth_g = depth_copies(stage_d1, land_d1, d1_send, d1_receive)
    for copy in depth_x + depth_g:
        copy.start()
    table_own(fields, tables)
    table_x[16] = jnp.zeros((64, 8, 128), F32)
    table_g[16] = jnp.zeros((64, 8, 128), F32)
    spread_word(round_sem, 0)
    for copy in depth_x:
        copy.wait()
    accept_depth((features,), land_d, sections, tables)
    stage_tile(1, sections, send_tile, stage_t)
    tile_x = tile_copies(stage_t, land_t, t_send, t_receive)
    for copy in tile_x:
        copy.start()
    table_depth(sections, tables[:1])
    spread_weight(first_weight, wide_first)
    for copy in depth_g:
        copy.wait()
    accept_depth((cotangent,), land_d1, sections1, tables)
    stage_tile(1, sections1, send_tile, stage_t1)
    tile_g = tile_copies(stage_t1, land_t1, t1_send, t1_receive)
    for copy in tile_g:
        copy.start()
    spread_word(round_sem, 1)
    table_depth(sections1, tables[1:])
    for copy in tile_x:
        copy.wait()
    table_tile(land_t, tables[:1])
    build_shifts(table_x, links, even_x, odd_x)
    spread_word(round_sem, 2)
    pre[...] = jnp.zeros((512, 256), F32)
    back[...] = jnp.zeros((512, 256), F32)
    conv_forward(even_x, odd_x, wide_first, pre)
    spread_word(round_sem, 3)
    spread_weight(second_weight, wide_second)
    value = pre[...]
    sigma = 1.0 / (1.0 + jnp.exp(-value))
    hidden[...] = (value * sigma).T.astype(BF16)
    pre[...] = sigma * (1.0 + value * (1.0 - sigma))
    for copy in tile_g:
        copy.wait()
    table_tile(land_t1, tables[1:])
    build_shifts(table_g, links, even_g, odd_g)
    spread_word(round_sem, 4)
    conv_backward(even_g, odd_g, wide_second, back)
    spread_word(round_sem, 5)
    grad_pre[...] = (back[...] * pre[...]).T.astype(BF16).reshape(8, 32, 512)

    stage_depth((grad_pre,), send_depth, stage_d2)
    along_depth = depth_copies(stage_d2, land_d2, d2_send, d2_receive)
    for copy in along_depth:
        copy.start()
    weight_gradient(lambda: hidden[...], even_g, odd_g, folded)
    spread_word(round_sem, 6)
    remotes, owns = share_workers(workers_in, names_land, n_send, n_receive, n_own)
    for copy in remotes + owns:
        copy.start()
    for copy in along_depth:
        copy.wait()
    accept_depth((grad_pre,), land_d2, sections2, tables)
    stage_tile(1, sections2, send_tile, stage_t2)
    along_tile = tile_copies(stage_t2, land_t2, t2_send, t2_receive)
    for copy in along_tile:
        copy.start()
    pack_gradient(folded, packed.at[1])
    plans = [
        reduce_plans(
            packed.at[w], land_a.at[w], part.at[w], land_b.at[w], result.at[w],
            tuple(s.at[w] for s in (a_send, a_receive, b_send, b_receive, c_send, c_receive)),
        )
        for w in range(2)
    ]
    start_all(plans[1][0])
    table_own((grad_pre,), tables[:1])
    table_depth(sections2, tables[:1])
    for copy in along_tile:
        copy.wait()
    table_tile(land_t2, tables[:1])
    build_shifts(table_x, links, even_x, odd_x)
    back[...] = jnp.zeros((512, 256), F32)
    conv_backward(even_x, odd_x, wide_first, back)
    grad_input[...] = (back[...].T.reshape(8, 32, 512) + cotangent[...].astype(F32)).astype(BF16)
    for step in (2, 1, 3):
        for axis in range(2):
            broadcast_copy(axis, step, grad_input, gather, g_send, g_receive).start()
    for axis in range(2):
        gather[axis, line_place(axis), 0:8] = grad_input[:, 16 * axis : 16 * axis + 16]
        for source in range(4):
            gather[axis, source, 8] = jnp.zeros((16, 512), BF16)
    all_names = all_of(names_land.at[pl.ds(0, 6)], n_send, n_receive)
    all_names.wait_recv()
    for copy in owns:
        copy.wait()
    to_scalar = pltpu.make_async_copy(names_land, names, n_sem)
    to_scalar.start()
    to_scalar.wait()
    find_slots(names, slots)

    factor = float(DEPTHS * TILES * 8 * 512) ** (-0.5)
    reduce_first(plans[1], packed.at[1], land_a.at[1], part.at[1], land_b.at[1])
    weight_gradient(lambda: features[...].reshape(256, 512), even_x, odd_x, folded)
    pack_gradient(folded, packed.at[0])
    start_all(plans[0][0])
    for axis in range(2):
        all_of(gather.at[axis, pl.ds(0, 3), pl.ds(0, 8)], g_send.at[axis], g_receive.at[axis]).wait_recv()
    parts = (gather, slots, outgoing, moved, m_send, m_receive, own_sem)
    send_messages((2,), *parts)
    reduce_second(plans[1], part.at[1], land_b.at[1], result.at[1], factor)
    reduce_first(plans[0], packed.at[0], land_a.at[0], part.at[0], land_b.at[0])
    send_messages((1, 3), *parts)
    wait_arrived(plans[1][2])
    unpack_gradient(result.at[1], gradients, 1)
    reduce_second(plans[0], part.at[0], land_b.at[0], result.at[0], factor)
    send_messages((0,), *parts)
    wait_arrived(plans[0][2])
    unpack_gradient(result.at[0], gradients, 0)
    store = pltpu.make_async_copy(gradients, gradients_out, store_sem)
    store.start()
    for w in range(2):
        for plan in plans[w]:
            wait_sent(plan)
    all_names.wait_send()
    for axis in range(2):
        all_of(gather.at[axis, pl.ds(0, 3), pl.ds(0, 8)], g_send.at[axis], g_receive.at[axis]).wait_send()
        pltpu.make_async_copy(outgoing.at[axis, 0], message_target(axis, moved), own_sem.at[axis]).wait()
        messages = all_of(outgoing.at[axis, pl.ds(1, 7)], m_send.at[axis], m_receive.at[axis])
        messages.wait_send()
        messages.wait_recv()
    store.wait()


def hand_over(moved_in, gradients_in, moved, gradients, held, held_gradients, in_sems, out_sems):
    spans = [(moved_in, held, moved, pl.ds(8 * i, 8)) for i in range(8)]
    spans += [(gradients_in, held_gradients, gradients, pl.ds(i, 1)) for i in range(2)]
    loads = [pltpu.make_async_copy(a.at[at], b.at[at], in_sems.at[i]) for i, (a, b, c, at) in enumerate(spans)]
    stores = [pltpu.make_async_copy(b.at[at], c.at[at], out_sems.at[i]) for i, (a, b, c, at) in enumerate(spans)]
    for load in loads:
        load.start()
    for load, store in zip(loads, stores):
        load.wait()
        store.start()
    for store in stores:
        store.wait()


def local(features, cotangent, first_weight, second_weight, neighbours, send_depth, send_tile, worker_tile):
    anywhere = pl.BlockSpec(memory_space=pl.ANY)
    brick = (32, 512)
    shifts = [pltpu.VMEM((3, 10, 80, 256), BF16), pltpu.VMEM((3, 10, 64, 256), BF16)]

    def halo(count):
        return [pltpu.VMEM((2, 2 * count, *brick), BF16)] * 4 + [pltpu.VMEM((count, 12, *brick), BF16)]

    dma = pltpu.SemaphoreType.DMA
    results = pl.pallas_call(
        kernel,
        out_shape=(
            jax.ShapeDtypeStruct((4, 4, 2, 2, *brick), BF16),
            jax.ShapeDtypeStruct((2, 27, 32, 32), F32),
        ),
        in_specs=[anywhere] * 8,
        out_specs=(anywhere, anywhere),
        scratch_shapes=[pltpu.VMEM((8, *brick), BF16)] * 2
        + [pltpu.VMEM((27, 32, 32), BF16)] * 2
        + [pltpu.SMEM((8, 26), jnp.int32), pltpu.SMEM((1, 2, 2), jnp.int32), pltpu.SMEM((1, 2, 2), jnp.int32)]
        + [pltpu.VMEM((2, 27, 32, 32), F32)]
        + [pltpu.VMEM((17, 64, 8, 128), F32)] * 2
        + shifts * 2
        + [pltpu.VMEM((3, 2304, 256), BF16)] * 2
        + [pltpu.VMEM((512, 256), F32)] * 2
        + [pltpu.VMEM((256, 512), BF16), pltpu.VMEM((864, 128), F32)]
        + [pltpu.VMEM((8, *brick), BF16), pltpu.VMEM((8, *brick), BF16)]
        + [pltpu.VMEM((2, 4, 9, 16, 512), BF16), pltpu.VMEM((2, 8, 4, 2, 16, 512), BF16)]
        + [pltpu.VMEM((8, 1, 8), jnp.int32), pltpu.SMEM((8, 1, 8), jnp.int32), pltpu.SMEM((8, 8), jnp.int32)]
        + halo(1)
        + halo(1)
        + halo(1)
        + [
            pltpu.VMEM((2, 32, 8, 128), F32),
            pltpu.VMEM((2, 8, 4, 8, 128), F32),
            pltpu.VMEM((2, 4, 8, 128), F32),
            pltpu.VMEM((2, 17, 4, 8, 128), F32),
            pltpu.VMEM((2, 32, 8, 128), F32),
        ]
        + [dma((2,))] * 12
        + [dma((7,)), dma]
        + [dma((2,))] * 5
        + [dma, dma, dma((2,)), dma]
        + [dma((2,))] * 6
        + [pltpu.SemaphoreType.REGULAR((6,))],
        compiler_params=pltpu.CompilerParams(
            collective_id=0, has_side_effects=True, vmem_limit_bytes=64 * 2**20 - 2**17
        ),
    )(features, cotangent, first_weight, second_weight, neighbours, send_depth, send_tile, worker_tile.reshape(1, 8))
    results = (results[0].reshape(2 * TILES, *brick), results[1])
    return pl.pallas_call(
        hand_over,
        out_shape=tuple(jax.ShapeDtypeStruct(r.shape, r.dtype) for r in results),
        in_specs=[anywhere] * 2,
        out_specs=(anywhere, anywhere),
        scratch_shapes=[pltpu.VMEM((2 * TILES, *brick), BF16), pltpu.VMEM((2, 27, 32, 32), F32), dma((10,)), dma((10,))],
        compiler_params=pltpu.CompilerParams(vmem_limit_bytes=64 * 2**20 - 2**17),
    )(*results)


def solution(mesh):
    rows = P(("depth", "tile"))
    placed = (rows, rows, P(), P(), rows, rows, rows, rows)
    return jax.shard_map(local, mesh=mesh, in_specs=placed, out_specs=(rows, P()), check_vma=False)
```
